256 devices in a mesh: stream: 4 (over x_lo, core), span: 64 (over z, y, x_hi).
Axes of the slice: x: 4 (x_hi: 2, x_lo: 2; x = x_hi * 2 + x_lo), y: 4, z: 8, core: 2. Of those that a mesh axis runs over, the one named last changes fastest.
Arguments:
- species: float32 [9, 32, 1024, 128], P(None, 'stream', 'span'), may hold values from 0 to 1
- flow: float32 [5, 32, 1024, 128], P(None, 'stream', 'span'), may hold values from -3 to 3
- interp_index: int32 [2, 128], replicated, may hold values from 0 to 126
- interp_frac: float32 [2, 128], replicated, may hold values from 0 to 1
- mean_gain: float32 [2, 14], replicated, may hold values from 1.5 to 4
- fluct_gain: float32 [2, 14], replicated, may hold values from 0.3 to 1
- reaction_table: int32 [21, 3], replicated, may hold values from 0 to 8
- rate_const: float32 [21], replicated, may hold values from 0.3 to 3
- activation: float32 [21], replicated, may hold values from 0.5 to 2
- heat_release: float32 [21], replicated, may hold values from 0.2 to 1
Outputs:
- species_next: float32 [9, 32, 1024, 128], P(None, 'stream', 'span')
- flow_next: float32 [5, 32, 1024, 128], P(None, 'stream', 'span')
The draws below stay inside these ranges and needn't reach their ends.
Inputs may be any that keep to these rules, and one draw needn't show every extreme that they name: `reaction_table`: a reactant may appear twice.
All inputs are finite; a program needn't handle non-finite values.
Results may differ from the reference program's by a relative error of at most 0.0003.
Values sent between devices are 32-bit elements; how exact they have to be, the bound alone decides.
A program may use at most 128 MiB of HBM per device.

```python
import math
import jax
import jax.numpy as jnp
from jax import lax

SPECIES = 9
FLOWS = 5
FIELDS = 14
REACT = 21
SX = 8
NY = 128
NX = 32
NZ = 1024


def plant(array, key, least, top_value):
    dims = array.shape
    spot = [jax.random.randint(jax.random.fold_in(key, axis), (), 0, dims[axis]) for axis in range(len(dims))]
    array = array.at[tuple(spot)].set(least)
    longest = dims.index(max(dims))
    spot[longest] = (spot[longest] + 1) % dims[longest]
    return array.at[tuple(spot)].set(top_value)


def level_of(rng, dims, split, least, top_value):
    factor_of = 1.0
    for axis_at, shards_of in split:
        draws = jax.random.uniform(jax.random.fold_in(jax.random.fold_in(rng, 6), axis_at), (shards_of,), jnp.float32, least / len(split), top_value / len(split))
        factor_of = factor_of * jnp.repeat(jnp.exp(draws), dims[axis_at] // shards_of).reshape((-1,) + (1,) * (len(dims) - 1 - axis_at))
    return factor_of


def bell_draw(stream_key, shape, width, most, split=(), kind=jnp.bfloat16):
    result = width * jax.random.normal(stream_key, shape, jnp.float32)
    if split:
        result = result * level_of(stream_key, shape, split, -0.22, 0.18)
    return jnp.clip(result, -most, most).astype(kind)


def setup_inputs(seed: int = 0) -> dict:
    keys = jax.random.split(jax.random.key(seed), 11)
    species = jnp.clip(1.0 * jax.random.uniform(keys[0], (SPECIES, NX, NZ, NY), jnp.float32) ** level_of(keys[0], (SPECIES, NX, NZ, NY), ((1, 4), (2, 64)), -0.2, 0.2), 0.0, 1.0)
    flow = bell_draw(keys[1], (FLOWS, NX, NZ, NY), 0.5, 3.0, ((1, 4), (2, 64)), jnp.float32)
    interp_index = plant(jax.random.randint(keys[2], (2, NY), 0, NY - 1), jax.random.fold_in(keys[2], 1), 0, (NY - 1) - 1).astype(jnp.int32)
    interp_frac = jnp.clip(jax.random.uniform(keys[3], (2, NY), jnp.float32, 0.0, 1.0), 0.0, 1.0)
    mean_gain = jnp.clip(jnp.exp(jax.random.uniform(keys[4], (2, FIELDS), jnp.float32, math.log(1.5), math.log(4.0))), 1.5, 4.0)
    fluct_gain = jnp.clip(jnp.exp(jax.random.uniform(keys[5], (2, FIELDS), jnp.float32, math.log(0.3), math.log(1.0))), 0.3, 1.0)
    reaction_table = plant(jax.random.randint(keys[6], (REACT, 3), 0, SPECIES), jax.random.fold_in(keys[6], 1), 0, SPECIES - 1).astype(jnp.int32)
    rate_const = jnp.clip(jnp.exp(jax.random.uniform(keys[7], (REACT,), jnp.float32, math.log(0.3), math.log(3.0))), 0.3, 3.0)
    activation = jnp.clip(jax.random.uniform(keys[8], (REACT,), jnp.float32, 0.5, 2.0), 0.5, 2.0)
    heat_release = jnp.clip(jax.random.uniform(keys[9], (REACT,), jnp.float32, 0.2, 1.0), 0.2, 1.0)
    return {"species": species, "flow": flow, "interp_index": interp_index, "interp_frac": interp_frac, "mean_gain": mean_gain, "fluct_gain": fluct_gain, "reaction_table": reaction_table, "rate_const": rate_const, "activation": activation, "heat_release": heat_release}


STENCIL = (0.8, -0.2, 4.0 / 105.0, -1.0 / 280.0)
TIMESTEP = 0.2
VISCOSITY = 0.1


def interpolate(values, index_row, frac_row):
    lower = jnp.take(values, index_row, axis=-1)
    upper = jnp.take(values, index_row + 1, axis=-1)
    return (1.0 - frac_row) * lower + frac_row * upper


def rescale(slab, mean, interp_index, interp_frac, mean_gain, fluct_gain):
    fluct = slab - mean[:, :, None, :]
    height = slab.shape[-1]
    levels = jnp.arange(height).astype(jnp.float32) / (height - 1.0)
    blend = 0.5 * (1.0 + jnp.tanh(6.0 * (levels - 0.5)))
    parts = []
    for branch in range(2):
        mean_part = interpolate(mean, interp_index[branch], interp_frac[branch])
        fluct_part = interpolate(fluct, interp_index[branch], interp_frac[branch])
        parts.append(mean_gain[branch][:, None, None, None] * mean_part[:, :, None, :]
                     + fluct_gain[branch][:, None, None, None] * fluct_part)
    return (1.0 - blend) * parts[0] + blend * parts[1]


def difference(padded, axis, count):
    total = jnp.zeros_like(lax.slice_in_dim(padded, 4, 4 + count, axis=axis))
    for offset in range(1, 5):
        ahead = lax.slice_in_dim(padded, 4 + offset, 4 + offset + count, axis=axis)
        behind = lax.slice_in_dim(padded, 4 - offset, 4 - offset + count, axis=axis)
        total = total + STENCIL[offset - 1] * (ahead - behind)
    return total


def tendency(state, ghosts, reaction_table, rate_const, activation, heat_release):
    zones = len(ghosts)
    slopes = []
    for zone in range(zones):
        block = state[:, zone * SX:(zone + 1) * SX]
        if zone + 1 < zones:
            after = state[:, (zone + 1) * SX:(zone + 1) * SX + 4]
        else:
            after = jnp.repeat(state[:, -1:], 4, axis=1)
        along = jnp.concatenate([ghosts[(zone - 1) % zones], block, after], 1)
        slopes.append(difference(along, 1, SX))
    slope_x = jnp.concatenate(slopes, 1)
    across = jnp.concatenate([state[:, :, -4:], state, state[:, :, :4]], 2)
    slope_z = difference(across, 2, state.shape[2])
    advection = (1.0 + state[9]) * slope_x + state[11] * slope_z
    floor_pad = jnp.zeros_like(state[..., :1])
    vertical = jnp.concatenate([floor_pad, state, state[..., -1:]], -1)
    curvature = vertical[..., 2:] - 2.0 * state + vertical[..., :-2]
    cold = jnp.exp(-state[13])
    labels = jnp.arange(SPECIES)
    spec_source = jnp.zeros_like(state[:SPECIES])
    heat_source = jnp.zeros_like(state[13])

    def react(counter, carry):
        spec_acc, heat_acc = carry
        first = jnp.take(state, reaction_table[counter, 0], axis=0)
        second = jnp.take(state, reaction_table[counter, 1], axis=0)
        rate = rate_const[counter] * jnp.exp(-activation[counter] * cold) * first * second
        weight = (2.0 * (labels == reaction_table[counter, 2]).astype(jnp.float32)
                  - (labels == reaction_table[counter, 0]).astype(jnp.float32)
                  - (labels == reaction_table[counter, 1]).astype(jnp.float32))
        return (spec_acc + weight[:, None, None, None] * rate[None], heat_acc + heat_release[counter] * rate)

    spec_source, heat_source = lax.fori_loop(0, REACT, react, (spec_source, heat_source))
    middle_zero = jnp.zeros_like(state[SPECIES:13])
    source = jnp.concatenate([spec_source, middle_zero, heat_source[None]], 0)
    return -advection + VISCOSITY * curvature + source


def reference(species, flow, interp_index, interp_frac, mean_gain, fluct_gain, reaction_table, rate_const, activation, heat_release):
    start = jnp.concatenate([species, flow], 0)
    ghosts = []
    for zone in range(NX // SX):
        first_plane = zone * SX + SX - 4
        slab = start[:, first_plane:first_plane + 4]
        mean = jnp.sum(slab, 2) / NZ
        ghosts.append(rescale(slab, mean, interp_index, interp_frac, mean_gain, fluct_gain))
    extra = (reaction_table, rate_const, activation, heat_release)
    lifted = start + TIMESTEP * tendency(start, ghosts, *extra)
    middle = 0.75 * start + 0.25 * (lifted + TIMESTEP * tendency(lifted, ghosts, *extra))
    final = start / 3.0 + (2.0 / 3.0) * (middle + TIMESTEP * tendency(middle, ghosts, *extra))
    return final[:SPECIES], final[SPECIES:]
```

```python
import functools

import jax
import jax.numpy as jnp
from jax import lax
from jax.experimental import pallas as pl
from jax.experimental.pallas import tpu as pltpu
from jax.sharding import PartitionSpec as P

MESH = pl.DeviceIdType.MESH
STENCIL = (0.8, -0.2, 4.0 / 105.0, -1.0 / 280.0)
TIMESTEP = 0.2
VISCOSITY = 0.1
SPECIES, FIELDS, REACT = 9, 14, 21
NY, ROWS, PLANES, HALF = 128, 16, 8, 4
TOP = 8
NZ_CHIPS, NY_CHIPS = 8, 4
YX_PEERS = [(dy, dx) for dy in range(4) for dx in range(2) if (dy, dx) != (0, 0)]
BLENDS = ((0.0, 1.0), (0.75, 0.25), (1.0 / 3.0, 2.0 / 3.0))


def own(h):
    return pl.ds(h * HALF, HALF)


def kernel(
    species_ref, flow_ref, index_ref, frac_ref, mean_gain, fluct_gain, table, rate_const, activation, heat,
    species_out, flow_out,
    x0, x1, x2, out_buf, follow, recycled, ghost, source, picked, weights, basis,
    sums, sums_in, part, part_in, mean_own, mean_in,
    load_sem, store_sem, z_send, z_recv, z0_send, z0_recv, f_send, f_recv, f0_send, f0_recv, r_send, r_recv,
    s_send, s_recv, p_send, p_recv, m_send, m_recv,
):
    stream, span = lax.axis_index("stream"), lax.axis_index("span")
    z, y, xh = span // 8, (span // 2) % 4, span % 2
    right, left = (stream, (span + 1) % 64), (stream, (span + 63) % 64)
    nxt, prev = ((stream + 1) % 4, span), ((stream + 3) % 4, span)
    first, last = stream == 0, stream == 3

    def along_z(group, d):
        return (group, ((z + d) % 8) * 8 + y * 2 + xh)

    def yx_peer(dy, dx):
        return (stream, z * 8 + ((y + dy) % 4) * 2 + (xh + dx) % 2)

    barrier = pltpu.get_barrier_semaphore()

    def hello(device):
        pl.semaphore_signal(barrier, inc=1, device_id=device, device_id_type=MESH)

    hello(left)
    hello(right)
    for d in range(8):
        hello(along_z((stream + 3) % 4, d))
    for d in range(1, 8):
        hello(along_z(stream, d))
    for dy, dx in YX_PEERS:
        hello(yx_peer(dy, dx))

    @pl.when(jnp.logical_not(last))
    def _():
        hello(nxt)

    loads = [
        pltpu.make_async_copy(species_ref, x0.at[pl.ds(0, SPECIES), :, pl.ds(TOP, ROWS)], load_sem.at[0]),
        pltpu.make_async_copy(flow_ref, x0.at[pl.ds(SPECIES, 5), :, pl.ds(TOP, ROWS)], load_sem.at[1]),
    ]
    for c in loads:
        c.start()

    def weight_row(r, _):
        a, b, p, k = table[r, 0], table[r, 1], table[r, 2], rate_const[r]
        for s in range(SPECIES):
            made = jnp.where(p == s, 2.0 * k, 0.0)
            weights[r, s] = made - jnp.where(a == s, k, 0.0) - jnp.where(b == s, k, 0.0)
        weights[r, SPECIES] = heat[r] * k
        return 0

    lax.fori_loop(0, REACT, weight_row, 0)

    pl.semaphore_wait(barrier, 2 + 8 + 7 + 7 + jnp.where(first, 0, 1))

    def remote(src, dst, send, recv, device):
        return pltpu.make_async_remote_copy(
            src_ref=src, dst_ref=dst, send_sem=send, recv_sem=recv, device_id=device, device_id_type=MESH
        )

    parts = ((species_ref, 0, SPECIES), (flow_ref, SPECIES, 5))

    def z0_copies(h):
        made = []
        for i, (ref, at, n) in enumerate(parts):
            made.append(remote(ref.at[:, own(h), pl.ds(0, 4)], x0.at[pl.ds(at, n), own(h), pl.ds(TOP + ROWS, 4)],
                               z0_send.at[h, i, 0], z0_recv.at[h, i, 0], left))
            made.append(remote(ref.at[:, own(h), pl.ds(ROWS - 4, 4)], x0.at[pl.ds(at, n), own(h), pl.ds(TOP - 4, 4)],
                               z0_send.at[h, i, 1], z0_recv.at[h, i, 1], right))
        return made

    def z_copies(buf, k, h):
        return [
            remote(buf.at[:, own(h), pl.ds(TOP, 4)], buf.at[:, own(h), pl.ds(TOP + ROWS, 4)],
                   z_send.at[k, h, 0], z_recv.at[k, h, 0], left),
            remote(buf.at[:, own(h), pl.ds(TOP + ROWS - 4, 4)], buf.at[:, own(h), pl.ds(TOP - 4, 4)],
                   z_send.at[k, h, 1], z_recv.at[k, h, 1], right),
        ]

    def f0_copies():
        return [
            remote(ref.at[:, own(0)], follow.at[0, pl.ds(at, n)], f0_send.at[i], f0_recv.at[i], prev)
            for i, (ref, at, n) in enumerate(parts)
        ]

    def f_copy(buf, k):
        return remote(buf.at[:, own(0), pl.ds(TOP, ROWS)], follow.at[k + 1], f_send.at[k], f_recv.at[k], prev)

    r_copies = [
        remote(ref.at[:, own(1)], recycled.at[pl.ds(at, n)], r_send.at[i], r_recv.at[i], nxt)
        for i, (ref, at, n) in enumerate(parts)
    ]
    for c in z0_copies(0) + r_copies:
        c.start()

    @pl.when(jnp.logical_not(first))
    def _():
        for c in f0_copies():
            c.start()

    for c in z0_copies(1):
        c.start()

    for c in loads:
        c.wait()

    def sum_rows(o, _):
        for i in range(2):
            for j in range(4):
                cells = x0[2 * o + i, HALF + j, pl.ds(TOP, ROWS), :]
                sums[o, pl.ds(4 * i + j, 1), :] = jnp.sum(cells, axis=0, keepdims=True)
        return 0

    lax.fori_loop(0, 7, sum_rows, 0)
    sums[7] = jnp.zeros((8, NY), jnp.float32)

    s_copies = [
        remote(sums.at[(z + d) % 8], sums_in.at[d - 1], s_send.at[d - 1], s_recv.at[d - 1], along_z(stream, d))
        for d in range(1, 8)
    ]
    for c in s_copies:
        c.start()

    lanes = lax.broadcasted_iota(jnp.int32, (8, NY), 1)
    bottom, top = lanes == 0, lanes == NY - 1

    def chemistry(buf, h):
        def pair(i, _):
            at = h * HALF + 2 * i
            cells = (pl.ds(at, 2), pl.ds(TOP, ROWS), slice(None))
            for s in range(SPECIES):
                picked[s] = buf[(s, *cells)]
            cold = jnp.exp(-buf[(13, *cells)])

            def react(t, acc):
                for u in range(3):
                    r = 3 * t + u
                    rate = jnp.exp(-activation[r] * cold) * picked[table[r, 0]] * picked[table[r, 1]]
                    acc = tuple(a + weights[r, s] * rate for s, a in enumerate(acc))
                return acc

            zero = jnp.zeros((2, ROWS, NY), jnp.float32)
            acc = lax.fori_loop(0, REACT // 3, react, (zero,) * 10)
            for s in range(SPECIES):
                source[s, pl.ds(at, 2)] = acc[s]
            for s in range(SPECIES, 13):
                source[s, pl.ds(at, 2)] = zero
            source[13, pl.ds(at, 2)] = acc[SPECIES]
            return 0

        lax.fori_loop(0, 2, pair, 0)

    def advance(buf, k, h, target, row0):
        before, after = BLENDS[k]

        def field(f, _):
            for t in range(2):
                at = TOP + 8 * t
                rows = pl.ds(at, 8)
                mine = [buf[f, p, rows, :] for p in range(PLANES)]
                side = [(ghost if h == 0 else follow.at[k])[f, j, pl.ds(8 * t, 8), :] for j in range(4)]
                line = side + mine if h == 0 else mine + side
                for q in range(HALF):
                    p, c = HALF * h + q, line[4 + q]
                    dx, dz = 0.0, 0.0
                    for o in range(1, 5):
                        dx = dx + STENCIL[o - 1] * (line[4 + q + o] - line[4 + q - o])
                        dz = dz + STENCIL[o - 1] * (buf[f, p, pl.ds(at + o, 8), :] - buf[f, p, pl.ds(at - o, 8), :])
                    down = jnp.where(bottom, 0.0, pltpu.roll(c, 1, 1))
                    up = jnp.where(top, c, pltpu.roll(c, NY - 1, 1))
                    slope = (1.0 + buf[9, p, rows, :]) * dx + buf[11, p, rows, :] * dz
                    change = VISCOSITY * (up - 2.0 * c + down) + source[f, p, pl.ds(8 * t, 8), :] - slope
                    value = after * (c + TIMESTEP * change)
                    if before:
                        value = value + before * x0[f, p, rows, :]
                    target[f, p, pl.ds(row0 + 8 * t, 8), :] = value
            return 0

        lax.fori_loop(0, FIELDS, field, 0)

    def repeat_last(buf, k):
        @pl.when(last)
        def _():
            def field(f, _):
                for j in range(4):
                    follow[k, f, j] = buf[f, PLANES - 1, pl.ds(TOP, ROWS), :]
                return 0

            lax.fori_loop(0, FIELDS, field, 0)

    level = lax.broadcasted_iota(jnp.int32, (1, NY), 1).astype(jnp.float32) / (NY - 1.0)
    blend = 0.5 * (1.0 + jnp.tanh(6.0 * (level - 0.5)))
    from_row = lax.broadcasted_iota(jnp.int32, (NY, NY), 0)
    for b, share in enumerate((1.0 - blend, blend)):
        index, frac = index_ref[pl.ds(b, 1), :], frac_ref[pl.ds(b, 1), :]
        lower = jnp.where(from_row == index, (1.0 - frac) * share, 0.0)
        basis[:, pl.ds(b * NY, NY)] = lower + jnp.where(from_row == index + 1, frac * share, 0.0)

    chemistry(x0, 0)

    for c in s_copies:
        c.wait()
    total = sums[z]
    for d in range(7):
        total = total + sums_in[d]
    part[...] = total
    p_copies = [
        remote(part, part_in.at[i], p_send.at[i], p_recv.at[i], yx_peer(dy, dx)) for i, (dy, dx) in enumerate(YX_PEERS)
    ]
    for c in p_copies:
        c.start()

    chemistry(x0, 1)
    repeat_last(x0, 0)

    for c in p_copies:
        c.wait()
    for i in range(7):
        total = total + part_in[i]
    mean_own[...] = total / 1024.0
    m_copies = [
        remote(mean_own, mean_in.at[z], m_send.at[d], m_recv.at[d], along_z((stream + 1) % 4, d)) for d in range(8)
    ]
    for c in m_copies:
        c.start()

    for c in r_copies:
        c.wait()

    def rescale_fluct(f, _):
        cells = recycled[f].reshape(4 * ROWS, NY)
        both = jnp.dot(cells, basis[...], precision=lax.Precision.HIGHEST, preferred_element_type=jnp.float32)
        value = fluct_gain[0, f] * both[:, :NY] + fluct_gain[1, f] * both[:, NY:]
        ghost[f] = value.reshape(4, ROWS, NY)
        return 0

    lax.fori_loop(0, FIELDS, rescale_fluct, 0)

    for c in m_copies:
        c.wait()

    def rescale_mean(o, _):
        both = jnp.dot(mean_in[o], basis[...], precision=lax.Precision.HIGHEST, preferred_element_type=jnp.float32)
        for i in range(2):
            f = 2 * o + i
            gain = [mean_gain[b, f] - fluct_gain[b, f] for b in range(2)]
            for j in range(4):
                row = both[4 * i + j:4 * i + j + 1]
                ghost[f, j] = ghost[f, j] + (gain[0] * row[:, :NY] + gain[1] * row[:, NY:])
        return 0

    lax.fori_loop(0, 7, rescale_mean, 0)

    def receive(copies):
        for c in copies:
            c.wait_recv()

    stores = []
    buffers = (x0, x1, x2)
    for k in range(3):
        buf = buffers[k]
        target, row0 = (buffers[k + 1], TOP) if k < 2 else (out_buf, 0)
        for h in range(2):
            receive(z0_copies(h) if k == 0 else z_copies(buf, k - 1, h))
            if h == 1:

                @pl.when(jnp.logical_not(last))
                def _():
                    receive(f0_copies() if k == 0 else [f_copy(buf, k - 1)])

            advance(buf, k, h, target, row0)
            if k < 2:
                for c in z_copies(target, k, h):
                    c.start()
                if h == 0:

                    @pl.when(jnp.logical_not(first))
                    def _():
                        f_copy(target, k).start()

                chemistry(target, h)
                if h == 1:
                    repeat_last(target, k + 1)
            else:
                for i, (ref, at, n) in enumerate(((species_out, 0, SPECIES), (flow_out, SPECIES, 5))):
                    c = pltpu.make_async_copy(out_buf.at[pl.ds(at, n), own(h)], ref.at[:, own(h)], store_sem.at[h, i])
                    c.start()
                    stores.append(c)

    for h in range(2):
        for c in z0_copies(h) + z_copies(x1, 0, h) + z_copies(x2, 1, h):
            c.wait_send()

    @pl.when(jnp.logical_not(first))
    def _():
        for c in f0_copies() + [f_copy(x1, 0), f_copy(x2, 1)]:
            c.wait_send()

    for c in stores:
        c.wait()


def on_device(species, flow, index, frac, mean_gain, fluct_gain, table, rate_const, activation, heat):
    vmem, smem, hbm = (pl.BlockSpec(memory_space=m) for m in (pltpu.VMEM, pltpu.SMEM, pl.ANY))
    f32, dma = jnp.float32, pltpu.SemaphoreType.DMA
    extended = pltpu.VMEM((FIELDS, PLANES, 2 * TOP + ROWS, NY), f32)
    scratch = [
        extended, extended, extended,
        pltpu.VMEM((FIELDS, PLANES, ROWS, NY), f32),
        pltpu.VMEM((3, FIELDS, HALF, ROWS, NY), f32),
        pltpu.VMEM((FIELDS, HALF, ROWS, NY), f32),
        pltpu.VMEM((FIELDS, HALF, ROWS, NY), f32),
        pltpu.VMEM((FIELDS, PLANES, ROWS, NY), f32),
        pltpu.VMEM((SPECIES, 2, ROWS, NY), f32),
        pltpu.SMEM((REACT, SPECIES + 1), f32),
        pltpu.VMEM((NY, 2 * NY), f32),
        pltpu.VMEM((8, 8, NY), f32),
        pltpu.VMEM((7, 8, NY), f32),
        pltpu.VMEM((8, NY), f32),
        pltpu.VMEM((7, 8, NY), f32),
        pltpu.VMEM((8, NY), f32),
        pltpu.VMEM((8, 8, NY), f32),
        dma((2,)), dma((2, 2)),
        dma((2, 2, 2)), dma((2, 2, 2)), dma((2, 2, 2)), dma((2, 2, 2)),
        dma((2,)), dma((2,)), dma((2,)), dma((2,)), dma((2,)), dma((2,)),
        dma((7,)), dma((7,)), dma((7,)), dma((7,)), dma((8,)), dma((8,)),
    ]
    return pl.pallas_call(
        kernel,
        out_shape=(jax.ShapeDtypeStruct(species.shape, f32), jax.ShapeDtypeStruct(flow.shape, f32)),
        in_specs=[hbm, hbm, vmem, vmem] + [smem] * 6,
        out_specs=(hbm, hbm),
        scratch_shapes=scratch,
        compiler_params=pltpu.CompilerParams(
            collective_id=0, has_side_effects=True, vmem_limit_bytes=40 * 1024 * 1024
        ),
    )(species, flow, index, frac, mean_gain, fluct_gain, table, rate_const, activation, heat)


def solution(mesh):
    split = P(None, "stream", "span", None)
    return jax.shard_map(
        on_device, mesh=mesh, in_specs=(split, split) + (P(),) * 8, out_specs=(split, split), check_vma=False
    )
```

```python
import functools

import jax
import jax.numpy as jnp
from jax import lax
from jax.experimental import pallas as pl
from jax.experimental.pallas import tpu as pltpu
from jax.sharding import PartitionSpec as P

MESH = pl.DeviceIdType.MESH
STENCIL = (0.8, -0.2, 4.0 / 105.0, -1.0 / 280.0)
TIMESTEP = 0.2
VISCOSITY = 0.1
SPECIES, FIELDS, REACT = 9, 14, 21
NY, ROWS, PLANES, HALF = 128, 16, 8, 4
TOP = 8
NZ_CHIPS, NY_CHIPS = 8, 4
YX_PEERS = [(dy, dx) for dy in range(4) for dx in range(2) if (dy, dx) != (0, 0)]
BLENDS = ((0.0, 1.0), (0.75, 0.25), (1.0 / 3.0, 2.0 / 3.0))


def own(h):
    return pl.ds(h * HALF, HALF)


def kernel(
    species_ref, flow_ref, index_ref, frac_ref, mean_gain, fluct_gain, table, rate_const, activation, heat,
    species_out, flow_out,
    x0, x1, x2, early, out_buf, follow, recycled, ghost, source, picked, weights, basis, pull,
    sums, sums_in, part, part_in, mean_own, mean_in,
    load_sem, store_sem, z_send, z_recv, z0_send, z0_recv, f_send, f_recv, f0_send, f0_recv, r_send, r_recv,
    s_send, s_recv, p_send, p_recv, m_send, m_recv,
):
    stream, span = lax.axis_index("stream"), lax.axis_index("span")
    z, y, xh = span // 8, (span // 2) % 4, span % 2
    right, left = (stream, (span + 1) % 64), (stream, (span + 63) % 64)
    nxt, prev = ((stream + 1) % 4, span), ((stream + 3) % 4, span)
    first, last = stream == 0, stream == 3

    def along_z(group, d):
        return (group, ((z + d) % 8) * 8 + y * 2 + xh)

    def yx_peer(dy, dx):
        return (stream, z * 8 + ((y + dy) % 4) * 2 + (xh + dx) % 2)

    barrier = pltpu.get_barrier_semaphore()

    def hello(device):
        pl.semaphore_signal(barrier, inc=1, device_id=device, device_id_type=MESH)

    hello(left)
    hello(right)
    for d in range(8):
        hello(along_z((stream + 3) % 4, d))
    for d in range(1, 8):
        hello(along_z(stream, d))
    for dy, dx in YX_PEERS:
        hello(yx_peer(dy, dx))

    @pl.when(jnp.logical_not(last))
    def _():
        hello(nxt)

    loads = [
        pltpu.make_async_copy(species_ref, x0.at[pl.ds(0, SPECIES), :, pl.ds(TOP, ROWS)], load_sem.at[0]),
        pltpu.make_async_copy(flow_ref, x0.at[pl.ds(SPECIES, 5), :, pl.ds(TOP, ROWS)], load_sem.at[1]),
    ]
    for c in loads:
        c.start()

    def weight_row(r, _):
        a, b, p, k = table[0, r], table[1, r], table[2, r], rate_const[r]
        for s in range(SPECIES):
            made = jnp.where(p == s, 2.0 * k, 0.0)
            weights[r, s] = made - jnp.where(a == s, k, 0.0) - jnp.where(b == s, k, 0.0)
        weights[r, SPECIES] = heat[r] * k
        return 0

    lax.fori_loop(0, REACT, weight_row, 0)

    pl.semaphore_wait(barrier, 2 + 8 + 7 + 7 + jnp.where(first, 0, 1))

    def remote(src, dst, send, recv, device):
        return pltpu.make_async_remote_copy(
            src_ref=src, dst_ref=dst, send_sem=send, recv_sem=recv, device_id=device, device_id_type=MESH
        )

    parts = ((species_ref, 0, SPECIES), (flow_ref, SPECIES, 5))

    def z0_copies(h):
        made = []
        for i, (ref, at, n) in enumerate(parts):
            made.append(remote(ref.at[:, own(h), pl.ds(0, 4)], x0.at[pl.ds(at, n), own(h), pl.ds(TOP + ROWS, 4)],
                               z0_send.at[h, i, 0], z0_recv.at[h, i, 0], left))
            made.append(remote(ref.at[:, own(h), pl.ds(ROWS - 4, 4)], x0.at[pl.ds(at, n), own(h), pl.ds(TOP - 4, 4)],
                               z0_send.at[h, i, 1], z0_recv.at[h, i, 1], right))
        return made

    def z_copies(buf, k, h):
        if (k, h) == (0, 0):
            buf = early
        return [
            remote(buf.at[:, own(h), pl.ds(TOP, 4)], buf.at[:, own(h), pl.ds(TOP + ROWS, 4)],
                   z_send.at[k, h, 0], z_recv.at[k, h, 0], left),
            remote(buf.at[:, own(h), pl.ds(TOP + ROWS - 4, 4)], buf.at[:, own(h), pl.ds(TOP - 4, 4)],
                   z_send.at[k, h, 1], z_recv.at[k, h, 1], right),
        ]

    def f0_copies():
        return [
            remote(ref.at[:, own(0)], follow.at[0, pl.ds(at, n)], f0_send.at[i], f0_recv.at[i], prev)
            for i, (ref, at, n) in enumerate(parts)
        ]

    def f_copy(buf, k):
        if k == 0:
            buf = early
        return remote(buf.at[:, own(0), pl.ds(TOP, ROWS)], follow.at[k + 1], f_send.at[k], f_recv.at[k], prev)

    r_copies = [
        remote(ref.at[:, own(1)], recycled.at[pl.ds(at, n)], r_send.at[i], r_recv.at[i], nxt)
        for i, (ref, at, n) in enumerate(parts)
    ]
    for c in z0_copies(0) + r_copies:
        c.start()

    @pl.when(jnp.logical_not(first))
    def _():
        for c in f0_copies():
            c.start()

    for c in z0_copies(1):
        c.start()

    for c in loads:
        c.wait()

    def sum_rows(o, _):
        for i in range(2):
            for j in range(4):
                cells = x0[2 * o + i, HALF + j, pl.ds(TOP, ROWS), :]
                sums[o, pl.ds(4 * i + j, 1), :] = jnp.sum(cells, axis=0, keepdims=True)
        return 0

    lax.fori_loop(0, 7, sum_rows, 0)
    sums[7] = jnp.zeros((8, NY), jnp.float32)

    s_copies = [
        remote(sums.at[(z + d) % 8], sums_in.at[d - 1], s_send.at[d - 1], s_recv.at[d - 1], along_z(stream, d))
        for d in range(1, 8)
    ]
    for c in s_copies:
        c.start()

    lanes = lax.broadcasted_iota(jnp.int32, (8, NY), 1)
    bottom, top = lanes == 0, lanes == NY - 1

    def chemistry(buf, h):
        def pair(i, _):
            at = h * HALF + 2 * i
            cells = (pl.ds(at, 2), pl.ds(TOP, ROWS), slice(None))
            for s in range(SPECIES):
                picked[s] = buf[(s, *cells)]
            cold = jnp.exp(-buf[(13, *cells)])

            def react(t, acc):
                for u in range(3):
                    r = 3 * t + u
                    rate = jnp.exp(-activation[r] * cold) * picked[table[0, r]] * picked[table[1, r]]
                    acc = tuple(a + weights[r, s] * rate for s, a in enumerate(acc))
                return acc

            zero = jnp.zeros((2, ROWS, NY), jnp.float32)
            acc = lax.fori_loop(0, REACT // 3, react, (zero,) * 10)
            for s in range(SPECIES):
                source[s, pl.ds(at, 2)] = acc[s]
            for s in range(SPECIES, 13):
                source[s, pl.ds(at, 2)] = zero
            source[13, pl.ds(at, 2)] = acc[SPECIES]
            return 0

        lax.fori_loop(0, 2, pair, 0)

    def advance(buf, k, h, target, row0):
        before, after = BLENDS[k]

        def field(f, _):
            for t in range(2):
                at = TOP + 8 * t
                rows = pl.ds(at, 8)
                mine = [buf[f, p, rows, :] for p in range(PLANES)]
                side = [(ghost if h == 0 else follow.at[k])[f, j, pl.ds(8 * t, 8), :] for j in range(4)]
                line = side + mine if h == 0 else mine + side
                for q in range(HALF):
                    p, c = HALF * h + q, line[4 + q]
                    dx, dz = 0.0, 0.0
                    for o in range(1, 5):
                        dx = dx + STENCIL[o - 1] * (line[4 + q + o] - line[4 + q - o])
                        dz = dz + STENCIL[o - 1] * (buf[f, p, pl.ds(at + o, 8), :] - buf[f, p, pl.ds(at - o, 8), :])
                    down = jnp.where(bottom, 0.0, pltpu.roll(c, 1, 1))
                    up = jnp.where(top, c, pltpu.roll(c, NY - 1, 1))
                    slope = (1.0 + buf[9, p, rows, :]) * dx + buf[11, p, rows, :] * dz
                    change = VISCOSITY * (up - 2.0 * c + down) + source[f, p, pl.ds(8 * t, 8), :] - slope
                    value = after * (c + TIMESTEP * change)
                    if before:
                        value = value + before * x0[f, p, rows, :]
                    target[f, p, pl.ds(row0 + 8 * t, 8), :] = value
            return 0

        lax.fori_loop(0, FIELDS, field, 0)

    def repeat_last(buf, k):
        @pl.when(last)
        def _():
            def field(f, _):
                for j in range(4):
                    follow[k, f, j] = buf[f, PLANES - 1, pl.ds(TOP, ROWS), :]
                return 0

            lax.fori_loop(0, FIELDS, field, 0)

    level = lax.broadcasted_iota(jnp.int32, (1, NY), 1).astype(jnp.float32) / (NY - 1.0)
    blend = 0.5 * (1.0 + jnp.tanh(6.0 * (level - 0.5)))
    from_row = lax.broadcasted_iota(jnp.int32, (NY, NY), 0)
    for b, share in enumerate((1.0 - blend, blend)):
        index, frac = index_ref[pl.ds(b, 1), :], frac_ref[pl.ds(b, 1), :]
        lower = jnp.where(from_row == index, (1.0 - frac) * share, 0.0)
        basis[:, pl.ds(b * NY, NY)] = lower + jnp.where(from_row == index + 1, frac * share, 0.0)

    chemistry(x0, 0)
    chemistry(x0, 1)
    repeat_last(x0, 0)

    for c in s_copies:
        c.wait()
    total = sums[z]
    for d in range(7):
        total = total + sums_in[d]
    part[...] = total
    p_copies = [
        remote(part, part_in.at[i], p_send.at[i], p_recv.at[i], yx_peer(dy, dx)) for i, (dy, dx) in enumerate(YX_PEERS)
    ]
    for c in p_copies:
        c.start()

    for c in r_copies:
        c.wait()

    def rescale_fluct(f, _):
        cells = recycled[f].reshape(4 * ROWS, NY)
        both = jnp.dot(cells, basis[...], precision=lax.Precision.HIGHEST, preferred_element_type=jnp.float32)
        value = fluct_gain[0, f] * both[:, :NY] + fluct_gain[1, f] * both[:, NY:]
        ghost[f] = value.reshape(4, ROWS, NY)
        return 0

    lax.fori_loop(0, FIELDS, rescale_fluct, 0)

    for c in p_copies:
        c.wait()
    for i in range(7):
        total = total + part_in[i]
    mean_own[...] = total / 1024.0
    mean_in[0, z] = mean_own[...]
    m_copies = [
        remote(mean_own, mean_in.at[1, z], m_send.at[d], m_recv.at[d], along_z((stream + 1) % 4, d)) for d in range(8)
    ] + [
        remote(mean_own, mean_in.at[0, z], m_send.at[7 + d], m_recv.at[7 + d], along_z(stream, d)) for d in range(1, 8)
    ]
    for c in m_copies:
        c.start()

    def rescale_mean(o, _):
        for w in range(2):
            both = jnp.dot(mean_in[w, o], basis[...], precision=lax.Precision.HIGHEST, preferred_element_type=jnp.float32)
            for i in range(2):
                f = 2 * o + i
                gain = [mean_gain[b, f] - fluct_gain[b, f] for b in range(2)]
                rows = both[4 * i:4 * i + 4]
                rows = gain[0] * rows[:, :NY] + gain[1] * rows[:, NY:]
                for q in range(HALF):
                    pull[w, f, pl.ds(q, 1), :] = sum(STENCIL[u - 1] * rows[4 + q - u:5 + q - u] for u in range(q + 1, 5))
                if w == 1:
                    for j in range(4):
                        ghost[f, j] = ghost[f, j] + rows[j:j + 1]
        return 0

    def correct_early():
        blocks = [pl.ds(TOP - 4 + 8 * t, 8) for t in range(3)]
        factor = [[TIMESTEP * (1.0 + x0[9, q, rows, :]) for rows in blocks] for q in range(HALF)]

        def field(f, _):
            for q in range(HALF):
                for t, rows in enumerate(blocks):
                    x1[f, q, rows, :] = early[f, q, rows, :] + factor[q][t] * pull[1, f, pl.ds(q, 1), :]
            return 0

        lax.fori_loop(0, FIELDS, field, 0)

    def correct_follow():
        @pl.when(jnp.logical_not(last))
        def _():
            factor = [TIMESTEP * (1.0 + follow[0, 9, q]) for q in range(HALF)]

            def field(f, _):
                for q in range(HALF):
                    follow[1, f, q] = follow[1, f, q] + factor[q] * pull[0, f, pl.ds(q, 1), :]
                return 0

            lax.fori_loop(0, FIELDS, field, 0)

    def receive(copies):
        for c in copies:
            c.wait_recv()

    stores = []
    buffers = (x0, x1, x2)
    for k in range(3):
        buf = buffers[k]
        target, row0 = (buffers[k + 1], TOP) if k < 2 else (out_buf, 0)
        for h in range(2):
            if (k, h) == (1, 0):
                for c in m_copies:
                    c.wait()
                lax.fori_loop(0, 7, rescale_mean, 0)
            receive(z0_copies(h) if k == 0 else z_copies(buf, k - 1, h))
            if (k, h) == (1, 0):
                correct_early()
                chemistry(x1, 0)
            if h == 1:

                @pl.when(jnp.logical_not(last))
                def _():
                    receive(f0_copies() if k == 0 else [f_copy(buf, k - 1)])

                if k == 1:
                    correct_follow()

            advance(buf, k, h, early if (k, h) == (0, 0) else target, row0)
            if k < 2:
                for c in z_copies(target, k, h):
                    c.start()
                if h == 0:

                    @pl.when(jnp.logical_not(first))
                    def _():
                        f_copy(target, k).start()

                if (k, h) != (0, 0):
                    chemistry(target, h)
                if h == 1:
                    repeat_last(target, k + 1)
            else:
                for i, (ref, at, n) in enumerate(((species_out, 0, SPECIES), (flow_out, SPECIES, 5))):
                    c = pltpu.make_async_copy(out_buf.at[pl.ds(at, n), own(h)], ref.at[:, own(h)], store_sem.at[h, i])
                    c.start()
                    stores.append(c)

    for h in range(2):
        for c in z0_copies(h) + z_copies(x1, 0, h) + z_copies(x2, 1, h):
            c.wait_send()

    @pl.when(jnp.logical_not(first))
    def _():
        for c in f0_copies() + [f_copy(x1, 0), f_copy(x2, 1)]:
            c.wait_send()

    for c in stores:
        c.wait()


def on_device(species, flow, index, frac, mean_gain, fluct_gain, table, rate_const, activation, heat):
    vmem, smem, hbm, anywhere = (pl.BlockSpec(memory_space=m) for m in (pltpu.VMEM, pltpu.SMEM, pltpu.HBM, pl.ANY))
    f32, dma = jnp.float32, pltpu.SemaphoreType.DMA
    extended = pltpu.VMEM((FIELDS, PLANES, 2 * TOP + ROWS, NY), f32)
    scratch = [
        extended, extended, extended,
        pltpu.VMEM((FIELDS, HALF, 2 * TOP + ROWS, NY), f32),
        pltpu.VMEM((FIELDS, PLANES, ROWS, NY), f32),
        pltpu.VMEM((3, FIELDS, HALF, ROWS, NY), f32),
        pltpu.VMEM((FIELDS, HALF, ROWS, NY), f32),
        pltpu.VMEM((FIELDS, HALF, ROWS, NY), f32),
        pltpu.VMEM((FIELDS, PLANES, ROWS, NY), f32),
        pltpu.VMEM((SPECIES, 2, ROWS, NY), f32),
        pltpu.SMEM((REACT, SPECIES + 1), f32),
        pltpu.VMEM((NY, 2 * NY), f32),
        pltpu.VMEM((2, FIELDS, HALF, NY), f32),
        pltpu.VMEM((8, 8, NY), f32),
        pltpu.VMEM((7, 8, NY), f32),
        pltpu.VMEM((8, NY), f32),
        pltpu.VMEM((7, 8, NY), f32),
        pltpu.VMEM((8, NY), f32),
        pltpu.VMEM((2, 8, 8, NY), f32),
        dma((2,)), dma((2, 2)),
        dma((2, 2, 2)), dma((2, 2, 2)), dma((2, 2, 2)), dma((2, 2, 2)),
        dma((2,)), dma((2,)), dma((2,)), dma((2,)), dma((2,)), dma((2,)),
        dma((7,)), dma((7,)), dma((7,)), dma((7,)), dma((15,)), dma((15,)),
    ]
    return pl.pallas_call(
        kernel,
        out_shape=(jax.ShapeDtypeStruct(species.shape, f32), jax.ShapeDtypeStruct(flow.shape, f32)),
        in_specs=[hbm, hbm, vmem, vmem] + [smem] * 6,
        out_specs=(anywhere, anywhere),
        scratch_shapes=scratch,
        compiler_params=pltpu.CompilerParams(
            collective_id=0, has_side_effects=True, vmem_limit_bytes=60 * 1024 * 1024
        ),
    )(species, flow, index, frac, mean_gain, fluct_gain, table.T, rate_const, activation, heat)


def solution(mesh):
    split = P(None, "stream", "span", None)
    return jax.shard_map(
        on_device, mesh=mesh, in_specs=(split, split) + (P(),) * 8, out_specs=(split, split), check_vma=False
    )
```

```python
import functools

import jax
import jax.numpy as jnp
from jax import lax
from jax.experimental import pallas as pl
from jax.experimental.pallas import tpu as pltpu
from jax.sharding import PartitionSpec as P

MESH = pl.DeviceIdType.MESH
STENCIL = (0.8, -0.2, 4.0 / 105.0, -1.0 / 280.0)
TIMESTEP = 0.2
VISCOSITY = 0.1
SPECIES, FIELDS, REACT = 9, 14, 21
NY, ROWS, PLANES, HALF = 128, 16, 8, 4
TOP = 8
BLENDS = ((0.0, 1.0), (0.75, 0.25), (1.0 / 3.0, 2.0 / 3.0))


def own(h):
    return pl.ds(h * HALF, HALF)


def kernel(
    species_ref, flow_ref, index_ref, frac_ref, mean_gain, fluct_gain, table, rate_const, activation, heat,
    species_out, flow_out,
    x0, x1, x2, early, follow, recycled, ghost, source, picked, weights, basis, pull,
    sums, raw_in, both_sums, sums_in, part, part_in, mean_own, mean_in, bounce,
    load_sem, z_send, z_recv, z0_send, z0_recv, f_send, f_recv, f0_send, f0_recv, r_send, r_recv,
    w_send, w_recv, s_send, s_recv, p_send, p_recv, m_send, m_recv, b_send, b_recv, o_send,
):
    stream, span = lax.axis_index("stream"), lax.axis_index("span")
    z, y, xh = span // 8, (span // 2) % 4, span % 2
    right, left = (stream, (span + 1) % 64), (stream, (span + 63) % 64)
    nxt, prev = ((stream + 1) % 4, span), ((stream + 3) % 4, span)
    first, last = stream == 0, stream == 3

    def along_z(group, d):
        return (group, ((z + d) % 8) * 8 + y * 2 + xh)

    def along_y(d):
        return (stream, z * 8 + ((y + d) % 4) * 2 + xh)

    def flip(group, at):
        return (group, at + 1 - 2 * (at % 2))

    barrier = pltpu.get_barrier_semaphore()

    def hello(device):
        pl.semaphore_signal(barrier, inc=1, device_id=device, device_id_type=MESH)

    hello(left)
    hello(right)
    hello(prev)
    hello(flip(prev[0], span))
    hello(flip(stream, span))
    for d in range(1, 8):
        hello(along_z(stream, d))
    for d in range(1, 4):
        hello(along_y(d))

    @pl.when(jnp.logical_not(last))
    def _():
        hello(nxt)

    loads = [
        pltpu.make_async_copy(species_ref, x0.at[pl.ds(0, SPECIES), :, pl.ds(TOP, ROWS)], load_sem.at[0]),
        pltpu.make_async_copy(flow_ref, x0.at[pl.ds(SPECIES, 5), :, pl.ds(TOP, ROWS)], load_sem.at[1]),
    ]
    for c in loads:
        c.start()

    def weight_row(r, _):
        a, b, p, k = table[0, r], table[1, r], table[2, r], rate_const[r]
        for s in range(SPECIES):
            made = jnp.where(p == s, 2.0 * k, 0.0)
            weights[r, s] = made - jnp.where(a == s, k, 0.0) - jnp.where(b == s, k, 0.0)
        weights[r, SPECIES] = heat[r] * k
        return 0

    lax.fori_loop(0, REACT, weight_row, 0)

    for c in loads:
        c.wait()

    def sum_rows(o, _):
        for i in range(2):
            for j in range(4):
                cells = x0[2 * o + i, HALF + j, pl.ds(TOP, ROWS), :]
                sums[o, pl.ds(4 * i + j, 1), :] = jnp.sum(cells, axis=0, keepdims=True)
        return 0

    lax.fori_loop(0, 7, sum_rows, 0)
    sums[7] = jnp.zeros((8, NY), jnp.float32)

    pl.semaphore_wait(barrier, 2 + 3 + 7 + 3 + jnp.where(first, 0, 1))

    def remote(src, dst, send, recv, device):
        return pltpu.make_async_remote_copy(
            src_ref=src, dst_ref=dst, send_sem=send, recv_sem=recv, device_id=device, device_id_type=MESH
        )

    parts = ((species_ref, 0, SPECIES), (flow_ref, SPECIES, 5))

    def z0_copies(h):
        return [
            remote(ref.at[:, own(h), pl.ds(0, 4)], x0.at[pl.ds(at, n), own(h), pl.ds(TOP + ROWS, 4)],
                   z0_send.at[h, i, 0], z0_recv.at[h, i, 0], left)
            for i, (ref, at, n) in enumerate(parts)
        ] + [
            remote(ref.at[:, own(h), pl.ds(ROWS - 4, 4)], x0.at[pl.ds(at, n), own(h), pl.ds(TOP - 4, 4)],
                   z0_send.at[h, i, 1], z0_recv.at[h, i, 1], right)
            for i, (ref, at, n) in enumerate(parts)
        ]

    def z_copies(buf, k, h):
        if (k, h) == (0, 0):
            buf = early
        return [
            remote(buf.at[:, own(h), pl.ds(TOP, 4)], buf.at[:, own(h), pl.ds(TOP + ROWS, 4)],
                   z_send.at[k, h, 0], z_recv.at[k, h, 0], left),
            remote(buf.at[:, own(h), pl.ds(TOP + ROWS - 4, 4)], buf.at[:, own(h), pl.ds(TOP - 4, 4)],
                   z_send.at[k, h, 1], z_recv.at[k, h, 1], right),
        ]

    def f0_copies():
        return [
            remote(ref.at[:, own(0)], follow.at[0, pl.ds(at, n)], f0_send.at[i], f0_recv.at[i], prev)
            for i, (ref, at, n) in enumerate(parts)
        ]

    def f_copy(buf, k):
        if k == 0:
            buf = early
        return remote(buf.at[:, own(0), pl.ds(TOP, ROWS)], follow.at[k + 1], f_send.at[k], f_recv.at[k], prev)

    r_copies = [
        remote(ref.at[:, own(1)], recycled.at[pl.ds(at, n)], r_send.at[i], r_recv.at[i], nxt)
        for i, (ref, at, n) in enumerate(parts)
    ]
    relay_copies = [
        remote(ref.at[:, own(1)], bounce.at[pl.ds(at, n)], b_send.at[i], b_recv.at[i], flip(0, span))
        for i, (ref, at, n) in enumerate(parts)
    ]
    onward_copies = [
        remote(bounce.at[pl.ds(at, n)], recycled.at[pl.ds(at, n)], o_send.at[i], r_recv.at[i], flip(0, span))
        for i, (ref, at, n) in enumerate(parts)
    ]
    raw_copies = [
        remote(sums, raw_in.at[i], w_send.at[i], w_recv.at[i], device)
        for i, device in enumerate((flip(stream, span), nxt, flip(nxt[0], span)))
    ]
    for c in raw_copies:
        c.start()

    def each_recycled(act):
        @pl.when(last)
        def _():
            for c in relay_copies:
                act(c)

        @pl.when(jnp.logical_not(last))
        def _():
            for c in r_copies:
                act(c)

    def start(c):
        c.start()

    each_recycled(start)

    @pl.when(jnp.logical_not(first))
    def _():
        for c in z0_copies(0):
            c.start()


    @pl.when(jnp.logical_not(first))
    def _():
        for c in f0_copies() + z0_copies(1):
            c.start()

    lanes = lax.broadcasted_iota(jnp.int32, (8, NY), 1)
    bottom, top = lanes == 0, lanes == NY - 1

    def chemistry(buf, h):
        def pair(i, _):
            at = h * HALF + 2 * i
            cells = (pl.ds(at, 2), pl.ds(TOP, ROWS), slice(None))
            for s in range(SPECIES):
                picked[s] = buf[(s, *cells)]
            cold = jnp.exp(-buf[(13, *cells)])

            def react(t, acc):
                for u in range(3):
                    r = 3 * t + u
                    rate = jnp.exp(-activation[r] * cold) * picked[table[0, r]] * picked[table[1, r]]
                    acc = tuple(a + weights[r, s] * rate for s, a in enumerate(acc))
                return acc

            zero = jnp.zeros((2, ROWS, NY), jnp.float32)
            acc = lax.fori_loop(0, REACT // 3, react, (zero,) * 10)
            for s in range(SPECIES):
                source[s, pl.ds(at, 2)] = acc[s]
            for s in range(SPECIES, 13):
                source[s, pl.ds(at, 2)] = zero
            source[13, pl.ds(at, 2)] = acc[SPECIES]
            return 0

        lax.fori_loop(0, 2, pair, 0)

    def advance(buf, k, h, store, fields=(0, FIELDS)):
        before, after = BLENDS[k]

        def field(f, _):
            for t in range(2):
                at = TOP + 8 * t
                rows = pl.ds(at, 8)
                mine = [buf[f, p, rows, :] for p in range(PLANES)]
                side = [(ghost if h == 0 else follow.at[k])[f, j, pl.ds(8 * t, 8), :] for j in range(4)]
                line = side + mine if h == 0 else mine + side
                for q in range(HALF):
                    p, c = HALF * h + q, line[4 + q]
                    dx, dz = 0.0, 0.0
                    for o in range(1, 5):
                        dx = dx + STENCIL[o - 1] * (line[4 + q + o] - line[4 + q - o])
                        dz = dz + STENCIL[o - 1] * (buf[f, p, pl.ds(at + o, 8), :] - buf[f, p, pl.ds(at - o, 8), :])
                    down = jnp.where(bottom, 0.0, pltpu.roll(c, 1, 1))
                    up = jnp.where(top, c, pltpu.roll(c, NY - 1, 1))
                    slope = (1.0 + buf[9, p, rows, :]) * dx + buf[11, p, rows, :] * dz
                    change = VISCOSITY * (up - 2.0 * c + down) + source[f, p, pl.ds(8 * t, 8), :] - slope
                    value = after * (c + TIMESTEP * change)
                    if before:
                        value = value + before * x0[f, p, rows, :]
                    store(f, p, t, value)
            return 0

        lax.fori_loop(*fields, field, 0)

    def repeat_last(buf, k):
        @pl.when(last)
        def _():
            def field(f, _):
                for j in range(4):
                    follow[k, f, j] = buf[f, PLANES - 1, pl.ds(TOP, ROWS), :]
                return 0

            lax.fori_loop(0, FIELDS, field, 0)

    level = lax.broadcasted_iota(jnp.int32, (1, NY), 1).astype(jnp.float32) / (NY - 1.0)
    blend = 0.5 * (1.0 + jnp.tanh(6.0 * (level - 0.5)))
    from_row = lax.broadcasted_iota(jnp.int32, (NY, NY), 0)
    for b, share in enumerate((1.0 - blend, blend)):
        index, frac = index_ref[pl.ds(b, 1), :], frac_ref[pl.ds(b, 1), :]
        lower = jnp.where(from_row == index, (1.0 - frac) * share, 0.0)
        basis[:, pl.ds(b * NY, NY)] = lower + jnp.where(from_row == index + 1, frac * share, 0.0)

    chemistry(x0, 0)
    for c in raw_copies:
        c.wait()
    both_sums[:, 0] = sums[...] + raw_in[0]
    both_sums[:, 1] = raw_in[1] + raw_in[2]
    s_copies = [
        remote(both_sums.at[(z + d) % 8], sums_in.at[d - 1], s_send.at[d - 1], s_recv.at[d - 1], along_z(stream, d))
        for d in range(1, 8)
    ]
    for c in s_copies:
        c.start()

    chemistry(x0, 1)
    repeat_last(x0, 0)

    @pl.when(first)
    def _():
        for a, b in zip(relay_copies, onward_copies):
            a.wait_recv()
            b.start()
        for c in z0_copies(0) + z0_copies(1):
            c.start()


    for c in s_copies:
        c.wait()
    total = both_sums[z]
    for d in range(7):
        total = total + sums_in[d]
    part[...] = total
    p_copies = [remote(part, part_in.at[d - 1], p_send.at[d - 1], p_recv.at[d - 1], along_y(d)) for d in range(1, 4)]
    for c in p_copies:
        c.start()

    for c in r_copies:
        c.wait_recv()

    for at in range(0, FIELDS, 7):
        cells = recycled[pl.ds(at, 7)].reshape(7 * 4 * ROWS, NY)
        both = jnp.dot(cells, basis[...], precision=lax.Precision.HIGHEST, preferred_element_type=jnp.float32)
        for i in range(7):
            value = both[i * 4 * ROWS:(i + 1) * 4 * ROWS]
            value = fluct_gain[0, at + i] * value[:, :NY] + fluct_gain[1, at + i] * value[:, NY:]
            ghost[at + i] = value.reshape(4, ROWS, NY)

    for c in p_copies:
        c.wait()
    for i in range(3):
        total = total + part_in[i]
    mean_own[...] = total / 1024.0
    mean_in[z] = mean_own[...]
    m_copies = [
        remote(mean_own, mean_in.at[z], m_send.at[d - 1], m_recv.at[d - 1], along_z(stream, d)) for d in range(1, 8)
    ]
    for c in m_copies:
        c.start()

    def rescale_mean(o, _):
        for w in range(2):
            both = jnp.dot(mean_in[o, w], basis[...], precision=lax.Precision.HIGHEST, preferred_element_type=jnp.float32)
            for i in range(2):
                f = 2 * o + i
                gain = [mean_gain[b, f] - fluct_gain[b, f] for b in range(2)]
                rows = both[4 * i:4 * i + 4]
                rows = gain[0] * rows[:, :NY] + gain[1] * rows[:, NY:]
                for q in range(HALF):
                    pull[w, f, pl.ds(q, 1), :] = sum(STENCIL[u - 1] * rows[4 + q - u:5 + q - u] for u in range(q + 1, 5))
                if w == 1:
                    for j in range(4):
                        ghost[f, j] = ghost[f, j] + rows[j:j + 1]
        return 0

    def correct_early():
        blocks = [pl.ds(TOP - 4 + 8 * t, 8) for t in range(3)]
        factor = [[TIMESTEP * (1.0 + x0[9, q, rows, :]) for rows in blocks] for q in range(HALF)]

        def field(f, _):
            for q in range(HALF):
                for t, rows in enumerate(blocks):
                    x1[f, q, rows, :] = early[f, q, rows, :] + factor[q][t] * pull[1, f, pl.ds(q, 1), :]
            return 0

        lax.fori_loop(0, FIELDS, field, 0)

    def correct_follow():
        @pl.when(jnp.logical_not(last))
        def _():
            factor = [TIMESTEP * (1.0 + follow[0, 9, q]) for q in range(HALF)]

            def field(f, _):
                for q in range(HALF):
                    follow[1, f, q] = follow[1, f, q] + factor[q] * pull[0, f, pl.ds(q, 1), :]
                return 0

            lax.fori_loop(0, FIELDS, field, 0)

    def receive(copies):
        for c in copies:
            c.wait_recv()

    buffers = (x0, x1, x2)
    for k in range(3):
        buf = buffers[k]
        target = buffers[k + 1] if k < 2 else None
        for h in range(2):
            if (k, h) == (1, 0):
                for c in m_copies:
                    c.wait()
                lax.fori_loop(0, 7, rescale_mean, 0)
            receive(z0_copies(h) if k == 0 else z_copies(buf, k - 1, h))
            if (k, h) == (1, 0):
                correct_early()
                chemistry(x1, 0)
            if h == 1:

                @pl.when(jnp.logical_not(last))
                def _():
                    receive(f0_copies() if k == 0 else [f_copy(buf, k - 1)])

                if k == 1:
                    correct_follow()

            if k < 2:
                into = early if (k, h) == (0, 0) else target

                def store(f, p, t, value):
                    into[f, p, pl.ds(TOP + 8 * t, 8), :] = value

                advance(buf, k, h, store)
                for c in z_copies(target, k, h):
                    c.start()
                if h == 0:

                    @pl.when(jnp.logical_not(first))
                    def _():
                        f_copy(target, k).start()

                if (k, h) != (0, 0):
                    chemistry(target, h)
                if h == 1:
                    repeat_last(target, k + 1)
            else:

                def store_species(f, p, t, value):
                    species_out[f, p, pl.ds(8 * t, 8), :] = value

                def store_flow(f, p, t, value):
                    flow_out[f - SPECIES, p, pl.ds(8 * t, 8), :] = value

                advance(buf, k, h, store_species, (0, SPECIES))
                advance(buf, k, h, store_flow, (SPECIES, FIELDS))

    for h in range(2):
        for c in z0_copies(h) + z_copies(x1, 0, h) + z_copies(x2, 1, h):
            c.wait_send()
    each_recycled(lambda c: c.wait_send())

    @pl.when(first)
    def _():
        for c in onward_copies:
            c.wait_send()

    @pl.when(jnp.logical_not(first))
    def _():
        for c in f0_copies() + [f_copy(x1, 0), f_copy(x2, 1)]:
            c.wait_send()


def on_device(species, flow, index, frac, mean_gain, fluct_gain, table, rate_const, activation, heat):
    vmem, smem, hbm = (pl.BlockSpec(memory_space=m) for m in (pltpu.VMEM, pltpu.SMEM, pltpu.HBM))
    f32, dma = jnp.float32, pltpu.SemaphoreType.DMA
    extended = pltpu.VMEM((FIELDS, PLANES, 2 * TOP + ROWS, NY), f32)
    scratch = [
        extended, extended, extended,
        pltpu.VMEM((FIELDS, HALF, 2 * TOP + ROWS, NY), f32),
        pltpu.VMEM((3, FIELDS, HALF, ROWS, NY), f32),
        pltpu.VMEM((FIELDS, HALF, ROWS, NY), f32),
        pltpu.VMEM((FIELDS, HALF, ROWS, NY), f32),
        pltpu.VMEM((FIELDS, PLANES, ROWS, NY), f32),
        pltpu.VMEM((SPECIES, 2, ROWS, NY), f32),
        pltpu.SMEM((REACT, SPECIES + 1), f32),
        pltpu.VMEM((NY, 2 * NY), f32),
        pltpu.VMEM((2, FIELDS, HALF, NY), f32),
        pltpu.VMEM((8, 8, NY), f32),
        pltpu.VMEM((3, 8, 8, NY), f32),
        pltpu.VMEM((8, 2, 8, NY), f32),
        pltpu.VMEM((7, 2, 8, NY), f32),
        pltpu.VMEM((2, 8, NY), f32),
        pltpu.VMEM((3, 2, 8, NY), f32),
        pltpu.VMEM((2, 8, NY), f32),
        pltpu.VMEM((8, 2, 8, NY), f32),
        pltpu.VMEM((FIELDS, HALF, ROWS, NY), f32),
        dma((2,)),
        dma((2, 2, 2)), dma((2, 2, 2)), dma((2, 2, 2)), dma((2, 2, 2)),
        dma((2,)), dma((2,)), dma((2,)), dma((2,)), dma((2,)), dma((2,)),
        dma((3,)), dma((3,)), dma((7,)), dma((7,)), dma((3,)), dma((3,)), dma((7,)), dma((7,)),
        dma((2,)), dma((2,)), dma((2,)),
    ]
    return pl.pallas_call(
        kernel,
        out_shape=(pltpu.VMEM(species.shape, f32), pltpu.VMEM(flow.shape, f32)),
        in_specs=[hbm, hbm, vmem, vmem] + [smem] * 6,
        out_specs=(vmem, vmem),
        scratch_shapes=scratch,
        compiler_params=pltpu.CompilerParams(
            collective_id=0, has_side_effects=True, vmem_limit_bytes=60 * 1024 * 1024
        ),
    )(species, flow, index, frac, mean_gain, fluct_gain, table.T, rate_const, activation, heat)


def solution(mesh):
    split = P(None, "stream", "span", None)
    return jax.shard_map(
        on_device, mesh=mesh, in_specs=(split, split) + (P(),) * 8, out_specs=(split, split), check_vma=False
    )
```

```python
import functools

import jax
import jax.numpy as jnp
from jax import lax
from jax.experimental import pallas as pl
from jax.experimental.pallas import tpu as pltpu
from jax.sharding import PartitionSpec as P

MESH = pl.DeviceIdType.MESH
STENCIL = (0.8, -0.2, 4.0 / 105.0, -1.0 / 280.0)
TIMESTEP = 0.2
VISCOSITY = 0.1
SPECIES, FIELDS, REACT = 9, 14, 21
NY, ROWS, PLANES, HALF = 128, 16, 8, 4
GATHER_Z, GATHER_Y = 5, 2
TOP = 8
BLENDS = ((0.0, 1.0), (0.75, 0.25), (1.0 / 3.0, 2.0 / 3.0))


def own(h):
    return pl.ds(h * HALF, HALF)


def kernel(
    species_ref, flow_ref, index_ref, frac_ref, mean_gain, fluct_gain, table, rate_const, activation, heat,
    species_out, flow_out,
    x0, x1, x2, early, follow, recycled, ghost, source, picked, weights, basis, pull,
    sums, raw_in, both_sums, sums_in, part, part_in, mean_own, mean_in, bounce,
    load_sem, z_send, z_recv, z0_send, z0_recv, f_send, f_recv, f0_send, f0_recv, r_send, r_recv,
    w_send, w_recv, s_send, s_recv, p_send, p_recv, m_send, m_recv, b_send, b_recv, o_send, all_here,
):
    stream, span = lax.axis_index("stream"), lax.axis_index("span")
    z, y, xh = span // 8, (span // 2) % 4, span % 2
    right, left = (stream, (span + 1) % 64), (stream, (span + 63) % 64)
    nxt, prev = ((stream + 1) % 4, span), ((stream + 3) % 4, span)
    first, last = stream == 0, stream == 3

    def along_z(group, d):
        return (group, ((z + d) % 8) * 8 + y * 2 + xh)

    def along_y(d):
        return (stream, z * 8 + ((y + d) % 4) * 2 + xh)

    def flip(group, at):
        return (group, at + 1 - 2 * (at % 2))

    gatherer = (stream, GATHER_Z * 8 + GATHER_Y * 2 + xh)
    gathers = span == gatherer[1]

    barrier = pltpu.get_barrier_semaphore()

    def hello(device):
        pl.semaphore_signal(barrier, inc=1, device_id=device, device_id_type=MESH)

    hello(left)
    hello(right)
    hello(prev)
    hello(flip(prev[0], span))
    hello(flip(stream, span))

    @pl.when(jnp.logical_not(gathers))
    def _():
        hello(gatherer)

    @pl.when(jnp.logical_not(last))
    def _():
        hello(nxt)

    loads = [
        pltpu.make_async_copy(species_ref, x0.at[pl.ds(0, SPECIES), :, pl.ds(TOP, ROWS)], load_sem.at[0]),
        pltpu.make_async_copy(flow_ref, x0.at[pl.ds(SPECIES, 5), :, pl.ds(TOP, ROWS)], load_sem.at[1]),
    ]
    for c in loads:
        c.start()

    def weight_row(r, _):
        a, b, p, k = table[0, r], table[1, r], table[2, r], rate_const[r]
        for s in range(SPECIES):
            made = jnp.where(p == s, 2.0 * k, 0.0)
            weights[r, s] = made - jnp.where(a == s, k, 0.0) - jnp.where(b == s, k, 0.0)
        weights[r, SPECIES] = heat[r] * k
        return 0

    lax.fori_loop(0, REACT, weight_row, 0)

    for c in loads:
        c.wait()

    def sum_rows(o, _):
        for i in range(2):
            for j in range(4):
                cells = x0[2 * o + i, HALF + j, pl.ds(TOP, ROWS), :]
                sums[o, pl.ds(4 * i + j, 1), :] = jnp.sum(cells, axis=0, keepdims=True)
        return 0

    lax.fori_loop(0, 7, sum_rows, 0)
    sums[7] = jnp.zeros((8, NY), jnp.float32)

    pl.semaphore_wait(barrier, 2 + 3 + jnp.where(first, 0, 1) + jnp.where(gathers, 31, 0))

    def remote(src, dst, send, recv, device):
        return pltpu.make_async_remote_copy(
            src_ref=src, dst_ref=dst, send_sem=send, recv_sem=recv, device_id=device, device_id_type=MESH
        )

    parts = ((species_ref, 0, SPECIES), (flow_ref, SPECIES, 5))

    def z0_copies(h):
        return [
            remote(ref.at[:, own(h), pl.ds(0, 4)], x0.at[pl.ds(at, n), own(h), pl.ds(TOP + ROWS, 4)],
                   z0_send.at[h, i, 0], z0_recv.at[h, i, 0], left)
            for i, (ref, at, n) in enumerate(parts)
        ] + [
            remote(ref.at[:, own(h), pl.ds(ROWS - 4, 4)], x0.at[pl.ds(at, n), own(h), pl.ds(TOP - 4, 4)],
                   z0_send.at[h, i, 1], z0_recv.at[h, i, 1], right)
            for i, (ref, at, n) in enumerate(parts)
        ]

    def z_copies(buf, k, h):
        if (k, h) == (0, 0):
            buf = early
        return [
            remote(buf.at[:, own(h), pl.ds(TOP, 4)], buf.at[:, own(h), pl.ds(TOP + ROWS, 4)],
                   z_send.at[k, h, 0], z_recv.at[k, h, 0], left),
            remote(buf.at[:, own(h), pl.ds(TOP + ROWS - 4, 4)], buf.at[:, own(h), pl.ds(TOP - 4, 4)],
                   z_send.at[k, h, 1], z_recv.at[k, h, 1], right),
        ]

    def f0_copies():
        return [
            remote(ref.at[:, own(0)], follow.at[0, pl.ds(at, n)], f0_send.at[i], f0_recv.at[i], prev)
            for i, (ref, at, n) in enumerate(parts)
        ]

    def f_copy(buf, k):
        if k == 0:
            buf = early
        return remote(buf.at[:, own(0), pl.ds(TOP, ROWS)], follow.at[k + 1], f_send.at[k], f_recv.at[k], prev)

    r_copies = [
        remote(ref.at[:, own(1)], recycled.at[pl.ds(at, n)], r_send.at[i], r_recv.at[i], nxt)
        for i, (ref, at, n) in enumerate(parts)
    ]
    relay_copies = [
        remote(ref.at[:, own(1)], bounce.at[pl.ds(at, n)], b_send.at[i], b_recv.at[i], flip(0, span))
        for i, (ref, at, n) in enumerate(parts)
    ]
    onward_copies = [
        remote(bounce.at[pl.ds(at, n)], recycled.at[pl.ds(at, n)], o_send.at[i], r_recv.at[i], flip(0, span))
        for i, (ref, at, n) in enumerate(parts)
    ]
    raw_copies = [
        remote(sums, raw_in.at[i], w_send.at[i], w_recv.at[i], device)
        for i, device in enumerate((flip(stream, span), nxt, flip(nxt[0], span)))
    ]
    for c in raw_copies:
        c.start()

    def each_recycled(act):
        @pl.when(last)
        def _():
            for c in relay_copies:
                act(c)

        @pl.when(jnp.logical_not(last))
        def _():
            for c in r_copies:
                act(c)

    def start(c):
        c.start()

    each_recycled(start)

    @pl.when(jnp.logical_not(first))
    def _():
        for c in z0_copies(0):
            c.start()


    @pl.when(jnp.logical_not(first))
    def _():
        for c in f0_copies() + z0_copies(1):
            c.start()

    @pl.when(gathers)
    def _():
        def tell(i, _):
            device = (stream, ((z + i // 4) % 8) * 8 + ((y + i % 4) % 4) * 2 + xh)
            pl.semaphore_signal(all_here, inc=1, device_id=device, device_id_type=MESH)
            return 0

        lax.fori_loop(1, 32, tell, 0)

    lanes = lax.broadcasted_iota(jnp.int32, (8, NY), 1)
    bottom, top = lanes == 0, lanes == NY - 1

    def chemistry(buf, h):
        def pair(i, _):
            at = h * HALF + 2 * i
            cells = (pl.ds(at, 2), pl.ds(TOP, ROWS), slice(None))
            for s in range(SPECIES):
                picked[s] = buf[(s, *cells)]
            cold = jnp.exp(-buf[(13, *cells)])

            def react(t, acc):
                for u in range(3):
                    r = 3 * t + u
                    rate = jnp.exp(-activation[r] * cold) * picked[table[0, r]] * picked[table[1, r]]
                    acc = tuple(a + weights[r, s] * rate for s, a in enumerate(acc))
                return acc

            zero = jnp.zeros((2, ROWS, NY), jnp.float32)
            acc = lax.fori_loop(0, REACT // 3, react, (zero,) * 10)
            for s in range(SPECIES):
                source[s, pl.ds(at, 2)] = acc[s]
            for s in range(SPECIES, 13):
                source[s, pl.ds(at, 2)] = zero
            source[13, pl.ds(at, 2)] = acc[SPECIES]
            return 0

        lax.fori_loop(0, 2, pair, 0)

    def advance(buf, k, h, store, fields=(0, FIELDS)):
        before, after = BLENDS[k]

        def field(f, _):
            for t in range(2):
                at = TOP + 8 * t
                rows = pl.ds(at, 8)
                mine = [buf[f, p, rows, :] for p in range(PLANES)]
                side = [(ghost if h == 0 else follow.at[k])[f, j, pl.ds(8 * t, 8), :] for j in range(4)]
                line = side + mine if h == 0 else mine + side
                for q in range(HALF):
                    p, c = HALF * h + q, line[4 + q]
                    dx, dz = 0.0, 0.0
                    for o in range(1, 5):
                        dx = dx + STENCIL[o - 1] * (line[4 + q + o] - line[4 + q - o])
                        dz = dz + STENCIL[o - 1] * (buf[f, p, pl.ds(at + o, 8), :] - buf[f, p, pl.ds(at - o, 8), :])
                    down = jnp.where(bottom, 0.0, pltpu.roll(c, 1, 1))
                    up = jnp.where(top, c, pltpu.roll(c, NY - 1, 1))
                    slope = (1.0 + buf[9, p, rows, :]) * dx + buf[11, p, rows, :] * dz
                    change = VISCOSITY * (up - 2.0 * c + down) + source[f, p, pl.ds(8 * t, 8), :] - slope
                    value = after * (c + TIMESTEP * change)
                    if before:
                        value = value + before * x0[f, p, rows, :]
                    store(f, p, t, value)
            return 0

        lax.fori_loop(*fields, field, 0)

    def repeat_last(buf, k):
        @pl.when(last)
        def _():
            def field(f, _):
                for j in range(4):
                    follow[k, f, j] = buf[f, PLANES - 1, pl.ds(TOP, ROWS), :]
                return 0

            lax.fori_loop(0, FIELDS, field, 0)

    level = lax.broadcasted_iota(jnp.int32, (1, NY), 1).astype(jnp.float32) / (NY - 1.0)
    blend = 0.5 * (1.0 + jnp.tanh(6.0 * (level - 0.5)))
    from_row = lax.broadcasted_iota(jnp.int32, (NY, NY), 0)
    for b, share in enumerate((1.0 - blend, blend)):
        index, frac = index_ref[pl.ds(b, 1), :], frac_ref[pl.ds(b, 1), :]
        lower = jnp.where(from_row == index, (1.0 - frac) * share, 0.0)
        basis[:, pl.ds(b * NY, NY)] = lower + jnp.where(from_row == index + 1, frac * share, 0.0)

    s_copies = [
        remote(both_sums.at[(z + d) % 8], sums_in.at[d - 1], s_send.at[d - 1], s_recv.at[d - 1], along_z(stream, d))
        for d in range(1, 8)
    ]
    p_copies = [remote(part, part_in.at[d - 1], p_send.at[d - 1], p_recv.at[d - 1], along_y(d)) for d in range(1, 4)]
    m_copies = [
        remote(mean_own, mean_in.at[z], m_send.at[d - 1], m_recv.at[d - 1], along_z(stream, d)) for d in range(1, 8)
    ]

    def sums_along_z():
        for c in raw_copies:
            c.wait()
        both_sums[:, 0] = sums[...] + raw_in[0]
        both_sums[:, 1] = raw_in[1] + raw_in[2]

        @pl.when(jnp.logical_not(gathers))
        def _():
            pl.semaphore_wait(all_here, 1)

        for c in s_copies:
            c.start()

    def sums_along_y():
        for c in s_copies:
            c.wait()
        total = both_sums[z]
        for d in range(7):
            total = total + sums_in[d]
        part[...] = total
        for c in p_copies:
            c.start()

    def hand_round():
        for c in p_copies:
            c.wait()
        total = part[...]
        for i in range(3):
            total = total + part_in[i]
        mean_own[...] = total / 1024.0
        mean_in[z] = mean_own[...]
        for c in m_copies:
            c.start()

    chemistry(x0, 0)
    chemistry(x0, 1)
    repeat_last(x0, 0)

    @pl.when(first)
    def _():
        for a, b in zip(relay_copies, onward_copies):
            a.wait_recv()
            b.start()
        for c in z0_copies(0) + z0_copies(1):
            c.start()

    sums_along_z()

    for c in r_copies:
        c.wait_recv()

    for at in range(0, FIELDS, 7):
        cells = recycled[pl.ds(at, 7)].reshape(7 * 4 * ROWS, NY)
        both = jnp.dot(cells, basis[...], precision=lax.Precision.HIGHEST, preferred_element_type=jnp.float32)
        for i in range(7):
            value = both[i * 4 * ROWS:(i + 1) * 4 * ROWS]
            value = fluct_gain[0, at + i] * value[:, :NY] + fluct_gain[1, at + i] * value[:, NY:]
            ghost[at + i] = value.reshape(4, ROWS, NY)

    def rescale_mean(o, _):
        for w in range(2):
            both = jnp.dot(mean_in[o, w], basis[...], precision=lax.Precision.HIGHEST, preferred_element_type=jnp.float32)
            for i in range(2):
                f = 2 * o + i
                gain = [mean_gain[b, f] - fluct_gain[b, f] for b in range(2)]
                rows = both[4 * i:4 * i + 4]
                rows = gain[0] * rows[:, :NY] + gain[1] * rows[:, NY:]
                for q in range(HALF):
                    pull[w, f, pl.ds(q, 1), :] = sum(STENCIL[u - 1] * rows[4 + q - u:5 + q - u] for u in range(q + 1, 5))
                if w == 1:
                    for j in range(4):
                        ghost[f, j] = ghost[f, j] + rows[j:j + 1]
        return 0

    def correct_early():
        blocks = [pl.ds(TOP - 4 + 8 * t, 8) for t in range(3)]
        factor = [[TIMESTEP * (1.0 + x0[9, q, rows, :]) for rows in blocks] for q in range(HALF)]

        def field(f, _):
            for q in range(HALF):
                for t, rows in enumerate(blocks):
                    x1[f, q, rows, :] = early[f, q, rows, :] + factor[q][t] * pull[1, f, pl.ds(q, 1), :]
            return 0

        lax.fori_loop(0, FIELDS, field, 0)

    def correct_follow():
        @pl.when(jnp.logical_not(last))
        def _():
            factor = [TIMESTEP * (1.0 + follow[0, 9, q]) for q in range(HALF)]

            def field(f, _):
                for q in range(HALF):
                    follow[1, f, q] = follow[1, f, q] + factor[q] * pull[0, f, pl.ds(q, 1), :]
                return 0

            lax.fori_loop(0, FIELDS, field, 0)

    def receive(copies):
        for c in copies:
            c.wait_recv()

    buffers = (x0, x1, x2)
    for k in range(3):
        buf = buffers[k]
        target = buffers[k + 1] if k < 2 else None
        for h in range(2):
            if (k, h) == (1, 0):
                for c in m_copies:
                    c.wait()
                lax.fori_loop(0, 7, rescale_mean, 0)
            receive(z0_copies(h) if k == 0 else z_copies(buf, k - 1, h))
            if (k, h) == (1, 0):
                correct_early()
                chemistry(x1, 0)
            if h == 1:

                @pl.when(jnp.logical_not(last))
                def _():
                    receive(f0_copies() if k == 0 else [f_copy(buf, k - 1)])

                if k == 1:
                    correct_follow()

            if k < 2:
                into = early if (k, h) == (0, 0) else target

                def store(f, p, t, value):
                    into[f, p, pl.ds(TOP + 8 * t, 8), :] = value

                advance(buf, k, h, store)
                for c in z_copies(target, k, h):
                    c.start()
                if h == 0:

                    @pl.when(jnp.logical_not(first))
                    def _():
                        f_copy(target, k).start()

                if (k, h) == (0, 0):
                    sums_along_y()
                    hand_round()
                if (k, h) != (0, 0):
                    chemistry(target, h)
                if h == 1:
                    repeat_last(target, k + 1)
            else:

                def store_species(f, p, t, value):
                    species_out[f, p, pl.ds(8 * t, 8), :] = value

                def store_flow(f, p, t, value):
                    flow_out[f - SPECIES, p, pl.ds(8 * t, 8), :] = value

                advance(buf, k, h, store_species, (0, SPECIES))
                advance(buf, k, h, store_flow, (SPECIES, FIELDS))

    for h in range(2):
        for c in z0_copies(h) + z_copies(x1, 0, h) + z_copies(x2, 1, h):
            c.wait_send()
    each_recycled(lambda c: c.wait_send())

    @pl.when(first)
    def _():
        for c in onward_copies:
            c.wait_send()

    @pl.when(jnp.logical_not(first))
    def _():
        for c in f0_copies() + [f_copy(x1, 0), f_copy(x2, 1)]:
            c.wait_send()


def on_device(species, flow, index, frac, mean_gain, fluct_gain, table, rate_const, activation, heat):
    vmem, smem, hbm = (pl.BlockSpec(memory_space=m) for m in (pltpu.VMEM, pltpu.SMEM, pltpu.HBM))
    f32, dma = jnp.float32, pltpu.SemaphoreType.DMA
    extended = pltpu.VMEM((FIELDS, PLANES, 2 * TOP + ROWS, NY), f32)
    scratch = [
        extended, extended, extended,
        pltpu.VMEM((FIELDS, HALF, 2 * TOP + ROWS, NY), f32),
        pltpu.VMEM((3, FIELDS, HALF, ROWS, NY), f32),
        pltpu.VMEM((FIELDS, HALF, ROWS, NY), f32),
        pltpu.VMEM((FIELDS, HALF, ROWS, NY), f32),
        pltpu.VMEM((FIELDS, PLANES, ROWS, NY), f32),
        pltpu.VMEM((SPECIES, 2, ROWS, NY), f32),
        pltpu.SMEM((REACT, SPECIES + 1), f32),
        pltpu.VMEM((NY, 2 * NY), f32),
        pltpu.VMEM((2, FIELDS, HALF, NY), f32),
        pltpu.VMEM((8, 8, NY), f32),
        pltpu.VMEM((3, 8, 8, NY), f32),
        pltpu.VMEM((8, 2, 8, NY), f32),
        pltpu.VMEM((7, 2, 8, NY), f32),
        pltpu.VMEM((2, 8, NY), f32),
        pltpu.VMEM((3, 2, 8, NY), f32),
        pltpu.VMEM((2, 8, NY), f32),
        pltpu.VMEM((8, 2, 8, NY), f32),
        pltpu.VMEM((FIELDS, HALF, ROWS, NY), f32),
        dma((2,)),
        dma((2, 2, 2)), dma((2, 2, 2)), dma((2, 2, 2)), dma((2, 2, 2)),
        dma((2,)), dma((2,)), dma((2,)), dma((2,)), dma((2,)), dma((2,)),
        dma((3,)), dma((3,)), dma((7,)), dma((7,)), dma((3,)), dma((3,)), dma((7,)), dma((7,)),
        dma((2,)), dma((2,)), dma((2,)), pltpu.SemaphoreType.REGULAR,
    ]
    return pl.pallas_call(
        kernel,
        out_shape=(pltpu.VMEM(species.shape, f32), pltpu.VMEM(flow.shape, f32)),
        in_specs=[hbm, hbm, vmem, vmem] + [smem] * 6,
        out_specs=(vmem, vmem),
        scratch_shapes=scratch,
        compiler_params=pltpu.CompilerParams(
            collective_id=0, has_side_effects=True, vmem_limit_bytes=60 * 1024 * 1024
        ),
    )(species, flow, index, frac, mean_gain, fluct_gain, table.T, rate_const, activation, heat)


def solution(mesh):
    split = P(None, "stream", "span", None)
    return jax.shard_map(
        on_device, mesh=mesh, in_specs=(split, split) + (P(),) * 8, out_specs=(split, split), check_vma=False
    )
```

```python
import functools

import jax
import jax.numpy as jnp
from jax import lax
from jax.experimental import pallas as pl
from jax.experimental.pallas import tpu as pltpu
from jax.sharding import PartitionSpec as P

MESH = pl.DeviceIdType.MESH
STENCIL = (0.8, -0.2, 4.0 / 105.0, -1.0 / 280.0)
TIMESTEP = 0.2
VISCOSITY = 0.1
SPECIES, FIELDS, REACT = 9, 14, 21
NY, ROWS, PLANES, HALF = 128, 16, 8, 4
GATHER_Z, GATHER_Y = 7, 2
TOP = 8
BLENDS = ((0.0, 1.0), (0.75, 0.25), (1.0 / 3.0, 2.0 / 3.0))


def own(h):
    return pl.ds(h * HALF, HALF)


def kernel(
    species_ref, flow_ref, index_hbm, frac_hbm, mean_gain_hbm, fluct_gain_hbm, table_hbm, rate_const_hbm, activation_hbm, heat_hbm,
    species_out, flow_out, index_ref, frac_ref, mean_gain, fluct_gain, table, rate_const, activation, heat,
    x0, x1, x2, early, follow, recycled, ghost, source, picked, weights, basis, pull,
    sums, raw_in, both_sums, sums_in, part, part_in, mean_own, mean_in, bounce,
    load_sem, small_sem, z_send, z_recv, z0_send, z0_recv, f_send, f_recv, f0_send, f0_recv, r_send, r_recv,
    w_send, w_recv, s_send, s_recv, p_send, p_recv, m_send, m_recv, b_send, b_recv, o_send, all_here,
):
    stream, span = lax.axis_index("stream"), lax.axis_index("span")
    z, y, xh = span // 8, (span // 2) % 4, span % 2
    right, left = (stream, (span + 1) % 64), (stream, (span + 63) % 64)
    nxt, prev = ((stream + 1) % 4, span), ((stream + 3) % 4, span)
    first, last = stream == 0, stream == 3

    def along_z(group, d):
        return (group, ((z + d) % 8) * 8 + y * 2 + xh)

    def along_y(d):
        return (stream, z * 8 + ((y + d) % 4) * 2 + xh)

    def flip(group, at):
        return (group, at + 1 - 2 * (at % 2))

    gatherer = (stream, GATHER_Z * 8 + GATHER_Y * 2 + xh)
    gathers = span == gatherer[1]

    barrier = pltpu.get_barrier_semaphore()

    def hello(device):
        pl.semaphore_signal(barrier, inc=1, device_id=device, device_id_type=MESH)

    hello(left)
    hello(right)
    hello(prev)
    hello(flip(prev[0], span))
    hello(flip(stream, span))

    @pl.when(jnp.logical_not(gathers))
    def _():
        hello(gatherer)

    @pl.when(jnp.logical_not(last))
    def _():
        hello(nxt)

    loads = [
        pltpu.make_async_copy(species_ref, x0.at[pl.ds(0, SPECIES), :, pl.ds(TOP, ROWS)], load_sem.at[0]),
        pltpu.make_async_copy(flow_ref, x0.at[pl.ds(SPECIES, 5), :, pl.ds(TOP, ROWS)], load_sem.at[1]),
    ]
    for c in loads:
        c.start()

    small_from = (index_hbm, frac_hbm, mean_gain_hbm, fluct_gain_hbm, table_hbm, rate_const_hbm, activation_hbm, heat_hbm)
    small_to = (index_ref, frac_ref, mean_gain, fluct_gain, table, rate_const, activation, heat)
    small = [pltpu.make_async_copy(a, b, small_sem.at[i]) for i, (a, b) in enumerate(zip(small_from, small_to))]
    for c in small:
        c.start()

    pl.semaphore_wait(barrier, 2 + 3 + jnp.where(first, 0, 1) + jnp.where(gathers, 31, 0))

    def remote(src, dst, send, recv, device):
        return pltpu.make_async_remote_copy(
            src_ref=src, dst_ref=dst, send_sem=send, recv_sem=recv, device_id=device, device_id_type=MESH
        )

    parts = ((species_ref, 0, SPECIES), (flow_ref, SPECIES, 5))

    def z0_copies(h):
        return [
            remote(ref.at[:, own(h), pl.ds(0, 4)], x0.at[pl.ds(at, n), own(h), pl.ds(TOP + ROWS, 4)],
                   z0_send.at[h, i, 0], z0_recv.at[h, i, 0], left)
            for i, (ref, at, n) in enumerate(parts)
        ] + [
            remote(ref.at[:, own(h), pl.ds(ROWS - 4, 4)], x0.at[pl.ds(at, n), own(h), pl.ds(TOP - 4, 4)],
                   z0_send.at[h, i, 1], z0_recv.at[h, i, 1], right)
            for i, (ref, at, n) in enumerate(parts)
        ]

    def z_copies(buf, k, h):
        if (k, h) == (0, 0):
            buf = early
        return [
            remote(buf.at[:, own(h), pl.ds(TOP, 4)], buf.at[:, own(h), pl.ds(TOP + ROWS, 4)],
                   z_send.at[k, h, 0], z_recv.at[k, h, 0], left),
            remote(buf.at[:, own(h), pl.ds(TOP + ROWS - 4, 4)], buf.at[:, own(h), pl.ds(TOP - 4, 4)],
                   z_send.at[k, h, 1], z_recv.at[k, h, 1], right),
        ]

    def f0_copies():
        return [
            remote(ref.at[:, own(0)], follow.at[0, pl.ds(at, n)], f0_send.at[i], f0_recv.at[i], prev)
            for i, (ref, at, n) in enumerate(parts)
        ]

    def f_copy(buf, k):
        if k == 0:
            buf = early
        return remote(buf.at[:, own(0), pl.ds(TOP, ROWS)], follow.at[k + 1], f_send.at[k], f_recv.at[k], prev)

    r_copies = [
        remote(ref.at[:, own(1)], recycled.at[pl.ds(at, n)], r_send.at[i], r_recv.at[i], nxt)
        for i, (ref, at, n) in enumerate(parts)
    ]
    relay_copies = [
        remote(ref.at[:, own(1)], bounce.at[pl.ds(at, n)], b_send.at[i], b_recv.at[i], flip(0, span))
        for i, (ref, at, n) in enumerate(parts)
    ]
    onward_copies = [
        remote(bounce.at[pl.ds(at, n)], recycled.at[pl.ds(at, n)], o_send.at[i], r_recv.at[i], flip(0, span))
        for i, (ref, at, n) in enumerate(parts)
    ]
    raw_copies = [
        remote(sums, raw_in.at[i], w_send.at[i], w_recv.at[i], device)
        for i, device in enumerate((flip(stream, span), nxt, flip(nxt[0], span)))
    ]
    def each_recycled(act):
        @pl.when(last)
        def _():
            for c in relay_copies:
                act(c)

        @pl.when(jnp.logical_not(last))
        def _():
            for c in r_copies:
                act(c)

    def start(c):
        c.start()

    for c in loads:
        c.wait()

    def sum_rows(o, _):
        for i in range(2):
            for j in range(4):
                cells = x0[2 * o + i, HALF + j, pl.ds(TOP, ROWS), :]
                sums[o, pl.ds(4 * i + j, 1), :] = jnp.sum(cells, axis=0, keepdims=True)
        return 0

    lax.fori_loop(0, 7, sum_rows, 0)
    sums[7] = jnp.zeros((8, NY), jnp.float32)

    for c in raw_copies:
        c.start()
    each_recycled(start)

    @pl.when(jnp.logical_not(first))
    def _():
        for c in z0_copies(0):
            c.start()

    @pl.when(jnp.logical_not(first))
    def _():
        for c in f0_copies() + z0_copies(1):
            c.start()

    @pl.when(gathers)
    def _():
        def tell(i, _):
            device = (stream, ((z + i // 4) % 8) * 8 + ((y + i % 4) % 4) * 2 + xh)
            pl.semaphore_signal(all_here, inc=1, device_id=device, device_id_type=MESH)
            return 0

        lax.fori_loop(1, 32, tell, 0)

    lanes = lax.broadcasted_iota(jnp.int32, (8, NY), 1)
    bottom, top = lanes == 0, lanes == NY - 1

    def chemistry(buf, h):
        def pair(i, _):
            at = h * HALF + 2 * i
            cells = (pl.ds(at, 2), pl.ds(TOP, ROWS), slice(None))
            for s in range(SPECIES):
                picked[s] = buf[(s, *cells)]
            cold = jnp.exp(-buf[(13, *cells)])

            def react(t, acc):
                for u in range(3):
                    r = 3 * t + u
                    rate = jnp.exp(-activation[r] * cold) * picked[table[0, r]] * picked[table[1, r]]
                    acc = tuple(a + weights[r, s] * rate for s, a in enumerate(acc))
                return acc

            zero = jnp.zeros((2, ROWS, NY), jnp.float32)
            acc = lax.fori_loop(0, REACT // 3, react, (zero,) * 10)
            for s in range(SPECIES):
                source[s, pl.ds(at, 2)] = acc[s]
            for s in range(SPECIES, 13):
                source[s, pl.ds(at, 2)] = zero
            source[13, pl.ds(at, 2)] = acc[SPECIES]
            return 0

        lax.fori_loop(0, 2, pair, 0)

    def advance(buf, k, h, store, fields=(0, FIELDS)):
        before, after = BLENDS[k]

        def field(f, _):
            for t in range(2):
                at = TOP + 8 * t
                rows = pl.ds(at, 8)
                mine = [buf[f, p, rows, :] for p in range(PLANES)]
                side = [(ghost if h == 0 else follow.at[k])[f, j, pl.ds(8 * t, 8), :] for j in range(4)]
                line = side + mine if h == 0 else mine + side
                for q in range(HALF):
                    p, c = HALF * h + q, line[4 + q]
                    dx, dz = 0.0, 0.0
                    for o in range(1, 5):
                        dx = dx + STENCIL[o - 1] * (line[4 + q + o] - line[4 + q - o])
                        dz = dz + STENCIL[o - 1] * (buf[f, p, pl.ds(at + o, 8), :] - buf[f, p, pl.ds(at - o, 8), :])
                    down = jnp.where(bottom, 0.0, pltpu.roll(c, 1, 1))
                    up = jnp.where(top, c, pltpu.roll(c, NY - 1, 1))
                    slope = (1.0 + buf[9, p, rows, :]) * dx + buf[11, p, rows, :] * dz
                    change = VISCOSITY * (up - 2.0 * c + down) + source[f, p, pl.ds(8 * t, 8), :] - slope
                    value = after * (c + TIMESTEP * change)
                    if before:
                        value = value + before * x0[f, p, rows, :]
                    store(f, p, t, value)
            return 0

        lax.fori_loop(*fields, field, 0)

    def repeat_last(buf, k):
        @pl.when(last)
        def _():
            def field(f, _):
                for j in range(4):
                    follow[k, f, j] = buf[f, PLANES - 1, pl.ds(TOP, ROWS), :]
                return 0

            lax.fori_loop(0, FIELDS, field, 0)

    for c in small:
        c.wait()

    def weight_row(r, _):
        a, b, p, k = table[0, r], table[1, r], table[2, r], rate_const[r]
        for s in range(SPECIES):
            made = jnp.where(p == s, 2.0 * k, 0.0)
            weights[r, s] = made - jnp.where(a == s, k, 0.0) - jnp.where(b == s, k, 0.0)
        weights[r, SPECIES] = heat[r] * k
        return 0

    lax.fori_loop(0, REACT, weight_row, 0)

    level = lax.broadcasted_iota(jnp.int32, (1, NY), 1).astype(jnp.float32) / (NY - 1.0)
    blend = 0.5 * (1.0 + jnp.tanh(6.0 * (level - 0.5)))
    from_row = lax.broadcasted_iota(jnp.int32, (NY, NY), 0)
    for b, share in enumerate((1.0 - blend, blend)):
        index, frac = index_ref[pl.ds(b, 1), :], frac_ref[pl.ds(b, 1), :]
        lower = jnp.where(from_row == index, (1.0 - frac) * share, 0.0)
        basis[:, pl.ds(b * NY, NY)] = lower + jnp.where(from_row == index + 1, frac * share, 0.0)

    s_copies = [
        remote(both_sums.at[(z + d) % 8], sums_in.at[d - 1], s_send.at[d - 1], s_recv.at[d - 1], along_z(stream, d))
        for d in range(1, 8)
    ]
    p_copies = [remote(part, part_in.at[d - 1], p_send.at[d - 1], p_recv.at[d - 1], along_y(d)) for d in range(1, 4)]
    m_copies = [
        remote(mean_own, mean_in.at[z], m_send.at[d - 1], m_recv.at[d - 1], along_z(stream, d)) for d in range(1, 8)
    ]

    def sums_along_z():
        for c in raw_copies:
            c.wait()
        both_sums[:, 0] = sums[...] + raw_in[0]
        both_sums[:, 1] = raw_in[1] + raw_in[2]

        @pl.when(jnp.logical_not(gathers))
        def _():
            pl.semaphore_wait(all_here, 1)

        for c in s_copies:
            c.start()

    def sums_along_y():
        for c in s_copies:
            c.wait()
        total = both_sums[z]
        for d in range(7):
            total = total + sums_in[d]
        part[...] = total
        for c in p_copies:
            c.start()

    def hand_round():
        for c in p_copies:
            c.wait()
        total = part[...]
        for i in range(3):
            total = total + part_in[i]
        mean_own[...] = total / 1024.0
        mean_in[z] = mean_own[...]
        for c in m_copies:
            c.start()

    chemistry(x0, 0)
    chemistry(x0, 1)
    repeat_last(x0, 0)

    @pl.when(first)
    def _():
        for a, b in zip(relay_copies, onward_copies):
            a.wait_recv()
            b.start()
        for c in z0_copies(0) + z0_copies(1):
            c.start()

    sums_along_z()

    for c in r_copies:
        c.wait_recv()

    for at in range(0, FIELDS, 7):
        cells = recycled[pl.ds(at, 7)].reshape(7 * 4 * ROWS, NY)
        both = jnp.dot(cells, basis[...], precision=lax.Precision.HIGHEST, preferred_element_type=jnp.float32)
        for i in range(7):
            value = both[i * 4 * ROWS:(i + 1) * 4 * ROWS]
            value = fluct_gain[0, at + i] * value[:, :NY] + fluct_gain[1, at + i] * value[:, NY:]
            ghost[at + i] = value.reshape(4, ROWS, NY)

    @pl.when(first)
    def _():
        sums_along_y()

    def rescale_mean(o, _):
        for w in range(2):
            both = jnp.dot(mean_in[o, w], basis[...], precision=lax.Precision.HIGHEST, preferred_element_type=jnp.float32)
            for i in range(2):
                f = 2 * o + i
                gain = [mean_gain[b, f] - fluct_gain[b, f] for b in range(2)]
                rows = both[4 * i:4 * i + 4]
                rows = gain[0] * rows[:, :NY] + gain[1] * rows[:, NY:]
                for q in range(HALF):
                    pull[w, f, pl.ds(q, 1), :] = sum(STENCIL[u - 1] * rows[4 + q - u:5 + q - u] for u in range(q + 1, 5))
                if w == 1:
                    for j in range(4):
                        ghost[f, j] = ghost[f, j] + rows[j:j + 1]
        return 0

    def correct_early():
        blocks = [pl.ds(TOP - 4 + 8 * t, 8) for t in range(3)]
        factor = [[TIMESTEP * (1.0 + x0[9, q, rows, :]) for rows in blocks] for q in range(HALF)]

        def field(f, _):
            for q in range(HALF):
                for t, rows in enumerate(blocks):
                    x1[f, q, rows, :] = early[f, q, rows, :] + factor[q][t] * pull[1, f, pl.ds(q, 1), :]
            return 0

        lax.fori_loop(0, FIELDS, field, 0)

    def correct_follow():
        @pl.when(jnp.logical_not(last))
        def _():
            factor = [TIMESTEP * (1.0 + follow[0, 9, q]) for q in range(HALF)]

            def field(f, _):
                for q in range(HALF):
                    follow[1, f, q] = follow[1, f, q] + factor[q] * pull[0, f, pl.ds(q, 1), :]
                return 0

            lax.fori_loop(0, FIELDS, field, 0)

    def receive(copies):
        for c in copies:
            c.wait_recv()

    buffers = (x0, x1, x2)
    for k in range(3):
        buf = buffers[k]
        target = buffers[k + 1] if k < 2 else None
        for h in range(2):
            if (k, h) == (1, 0):
                for c in m_copies:
                    c.wait()
                lax.fori_loop(0, 7, rescale_mean, 0)
            receive(z0_copies(h) if k == 0 else z_copies(buf, k - 1, h))
            if (k, h) == (1, 0):
                correct_early()
                chemistry(x1, 0)
            if h == 1:

                @pl.when(jnp.logical_not(last))
                def _():
                    receive(f0_copies() if k == 0 else [f_copy(buf, k - 1)])

                if k == 1:
                    correct_follow()

            if k < 2:
                into = early if (k, h) == (0, 0) else target

                def store(f, p, t, value):
                    into[f, p, pl.ds(TOP + 8 * t, 8), :] = value

                advance(buf, k, h, store)
                for c in z_copies(target, k, h):
                    c.start()
                if h == 0:

                    @pl.when(jnp.logical_not(first))
                    def _():
                        f_copy(target, k).start()

                if (k, h) == (0, 0):

                    @pl.when(jnp.logical_not(first))
                    def _():
                        sums_along_y()

                    hand_round()
                if (k, h) != (0, 0):
                    chemistry(target, h)
                if h == 1:
                    repeat_last(target, k + 1)
            else:

                def store_species(f, p, t, value):
                    species_out[f, p, pl.ds(8 * t, 8), :] = value

                def store_flow(f, p, t, value):
                    flow_out[f - SPECIES, p, pl.ds(8 * t, 8), :] = value

                advance(buf, k, h, store_species, (0, SPECIES))
                advance(buf, k, h, store_flow, (SPECIES, FIELDS))

    for h in range(2):
        for c in z0_copies(h) + z_copies(x1, 0, h) + z_copies(x2, 1, h):
            c.wait_send()
    each_recycled(lambda c: c.wait_send())

    @pl.when(first)
    def _():
        for c in onward_copies:
            c.wait_send()

    @pl.when(jnp.logical_not(first))
    def _():
        for c in f0_copies() + [f_copy(x1, 0), f_copy(x2, 1)]:
            c.wait_send()


def hand_out(species, flow, species_out, flow_out, sem):
    copies = [
        pltpu.make_async_copy(a.at[:, own(h)], b.at[:, own(h)], sem.at[i, h])
        for i, (a, b) in enumerate(((species, species_out), (flow, flow_out)))
        for h in range(2)
    ]
    for c in copies:
        c.start()
    for c in copies:
        c.wait()


def on_device(species, flow, index, frac, mean_gain, fluct_gain, table, rate_const, activation, heat):
    vmem, hbm = (pl.BlockSpec(memory_space=m) for m in (pltpu.VMEM, pltpu.HBM))
    f32, dma = jnp.float32, pltpu.SemaphoreType.DMA
    extended = pltpu.VMEM((FIELDS, PLANES, 2 * TOP + ROWS, NY), f32)
    small = (index, frac, mean_gain, fluct_gain, table.T, rate_const, activation, heat)
    scratch = [(pltpu.VMEM if i < 2 else pltpu.SMEM)(a.shape, a.dtype) for i, a in enumerate(small)]
    scratch += [
        extended, extended, extended,
        pltpu.VMEM((FIELDS, HALF, 2 * TOP + ROWS, NY), f32),
        pltpu.VMEM((3, FIELDS, HALF, ROWS, NY), f32),
        pltpu.VMEM((FIELDS, HALF, ROWS, NY), f32),
        pltpu.VMEM((FIELDS, HALF, ROWS, NY), f32),
        pltpu.VMEM((FIELDS, PLANES, ROWS, NY), f32),
        pltpu.VMEM((SPECIES, 2, ROWS, NY), f32),
        pltpu.SMEM((REACT, SPECIES + 1), f32),
        pltpu.VMEM((NY, 2 * NY), f32),
        pltpu.VMEM((2, FIELDS, HALF, NY), f32),
        pltpu.VMEM((8, 8, NY), f32),
        pltpu.VMEM((3, 8, 8, NY), f32),
        pltpu.VMEM((8, 2, 8, NY), f32),
        pltpu.VMEM((7, 2, 8, NY), f32),
        pltpu.VMEM((2, 8, NY), f32),
        pltpu.VMEM((3, 2, 8, NY), f32),
        pltpu.VMEM((2, 8, NY), f32),
        pltpu.VMEM((8, 2, 8, NY), f32),
        pltpu.VMEM((FIELDS, HALF, ROWS, NY), f32),
        dma((2,)), dma((8,)),
        dma((2, 2, 2)), dma((2, 2, 2)), dma((2, 2, 2)), dma((2, 2, 2)),
        dma((2,)), dma((2,)), dma((2,)), dma((2,)), dma((2,)), dma((2,)),
        dma((3,)), dma((3,)), dma((7,)), dma((7,)), dma((3,)), dma((3,)), dma((7,)), dma((7,)),
        dma((2,)), dma((2,)), dma((2,)), pltpu.SemaphoreType.REGULAR,
    ]
    results = pl.pallas_call(
        kernel,
        out_shape=(pltpu.VMEM(species.shape, f32), pltpu.VMEM(flow.shape, f32)),
        in_specs=[hbm] * 10,
        out_specs=(vmem, vmem),
        scratch_shapes=scratch,
        compiler_params=pltpu.CompilerParams(
            collective_id=0, has_side_effects=True, vmem_limit_bytes=60 * 1024 * 1024
        ),
    )(species, flow, *small)
    return pl.pallas_call(
        hand_out,
        out_shape=tuple(jax.ShapeDtypeStruct(a.shape, f32) for a in results),
        in_specs=[vmem] * 2,
        out_specs=(hbm, hbm),
        scratch_shapes=[dma((2, 2))],
    )(*(pltpu.with_memory_space_constraint(a, pltpu.VMEM) for a in results))


def solution(mesh):
    split = P(None, "stream", "span", None)
    return jax.shard_map(
        on_device, mesh=mesh, in_specs=(split, split) + (P(),) * 8, out_specs=(split, split), check_vma=False
    )
```

```python
import functools

import jax
import jax.numpy as jnp
from jax import lax
from jax.experimental import pallas as pl
from jax.experimental.pallas import tpu as pltpu
from jax.sharding import PartitionSpec as P

MESH = pl.DeviceIdType.MESH
STENCIL = (0.8, -0.2, 4.0 / 105.0, -1.0 / 280.0)
TIMESTEP = 0.2
VISCOSITY = 0.1
SPECIES, FIELDS, REACT = 9, 14, 21
NY, ROWS, PLANES, HALF = 128, 16, 8, 4
GATHER_Z, GATHER_Y = 7, 2
TOP = 8
BLENDS = ((0.0, 1.0), (0.75, 0.25), (1.0 / 3.0, 2.0 / 3.0))


def own(h):
    return pl.ds(h * HALF, HALF)


def kernel(
    species_ref, flow_ref, index_hbm, frac_hbm, mean_gain_hbm, fluct_gain_hbm, table_hbm, rate_const_hbm, activation_hbm, heat_hbm,
    species_out, flow_out, index_ref, frac_ref, mean_gain, fluct_gain, table, rate_const, activation, heat,
    x0, x1, x2, early, follow, recycled, ghost, source, picked, weights, basis, pull,
    sums, raw_in, both_sums, sums_in, part, part_in, mean_own, mean_in, bounce,
    load_sem, small_sem, z_send, z_recv, z0_send, z0_recv, f_send, f_recv, f0_send, f0_recv, r_send, r_recv,
    w_send, w_recv, s_send, s_recv, p_send, p_recv, m_send, m_recv, b_send, b_recv, o_send, all_here,
):
    stream, span = lax.axis_index("stream"), lax.axis_index("span")
    z, y, xh = span // 8, (span // 2) % 4, span % 2
    right, left = (stream, (span + 1) % 64), (stream, (span + 63) % 64)
    nxt, prev = ((stream + 1) % 4, span), ((stream + 3) % 4, span)
    first, last = stream == 0, stream == 3

    def along_z(group, d):
        return (group, ((z + d) % 8) * 8 + y * 2 + xh)

    def along_y(d):
        return (stream, z * 8 + ((y + d) % 4) * 2 + xh)

    def flip(group, at):
        return (group, at + 1 - 2 * (at % 2))

    gatherer = (stream, GATHER_Z * 8 + GATHER_Y * 2 + xh)
    gathers = span == gatherer[1]

    barrier = pltpu.get_barrier_semaphore()

    def hello(device):
        pl.semaphore_signal(barrier, inc=1, device_id=device, device_id_type=MESH)

    hello(left)
    hello(right)
    hello(prev)
    hello(flip(prev[0], span))
    hello(flip(stream, span))

    @pl.when(jnp.logical_not(gathers))
    def _():
        hello(gatherer)

    @pl.when(jnp.logical_not(last))
    def _():
        hello(nxt)

    loads = [
        pltpu.make_async_copy(species_ref, x0.at[pl.ds(0, SPECIES), :, pl.ds(TOP, ROWS)], load_sem.at[0]),
        pltpu.make_async_copy(flow_ref, x0.at[pl.ds(SPECIES, 5), :, pl.ds(TOP, ROWS)], load_sem.at[1]),
    ]
    for c in loads:
        c.start()

    small_from = (index_hbm, frac_hbm, mean_gain_hbm, fluct_gain_hbm, table_hbm, rate_const_hbm, activation_hbm, heat_hbm)
    small_to = (index_ref, frac_ref, mean_gain, fluct_gain, table, rate_const, activation, heat)
    small = [pltpu.make_async_copy(a, b, small_sem.at[i]) for i, (a, b) in enumerate(zip(small_from, small_to))]
    for c in small:
        c.start()

    pl.semaphore_wait(barrier, 2 + 3 + jnp.where(first, 0, 1) + jnp.where(gathers, 31, 0))

    def remote(src, dst, send, recv, device):
        return pltpu.make_async_remote_copy(
            src_ref=src, dst_ref=dst, send_sem=send, recv_sem=recv, device_id=device, device_id_type=MESH
        )

    parts = ((species_ref, 0, SPECIES), (flow_ref, SPECIES, 5))

    def z0_copies(h):
        return [
            remote(ref.at[:, own(h), pl.ds(0, 4)], x0.at[pl.ds(at, n), own(h), pl.ds(TOP + ROWS, 4)],
                   z0_send.at[h, i, 0], z0_recv.at[h, i, 0], left)
            for i, (ref, at, n) in enumerate(parts)
        ] + [
            remote(ref.at[:, own(h), pl.ds(ROWS - 4, 4)], x0.at[pl.ds(at, n), own(h), pl.ds(TOP - 4, 4)],
                   z0_send.at[h, i, 1], z0_recv.at[h, i, 1], right)
            for i, (ref, at, n) in enumerate(parts)
        ]

    def z_copies(buf, k, h):
        if (k, h) == (0, 0):
            buf = early
        return [
            remote(buf.at[:, own(h), pl.ds(TOP + ROWS - 4, 4)], buf.at[:, own(h), pl.ds(TOP - 4, 4)],
                   z_send.at[k, h, 1], z_recv.at[k, h, 1], right),
            remote(buf.at[:, own(h), pl.ds(TOP, 4)], buf.at[:, own(h), pl.ds(TOP + ROWS, 4)],
                   z_send.at[k, h, 0], z_recv.at[k, h, 0], left),
        ]

    def f0_copies():
        return [
            remote(ref.at[:, own(0)], follow.at[0, pl.ds(at, n)], f0_send.at[i], f0_recv.at[i], prev)
            for i, (ref, at, n) in enumerate(parts)
        ]

    def f_copy(buf, k):
        if k == 0:
            buf = early
        return remote(buf.at[:, own(0), pl.ds(TOP, ROWS)], follow.at[k + 1], f_send.at[k], f_recv.at[k], prev)

    r_copies = [
        remote(ref.at[:, own(1)], recycled.at[pl.ds(at, n)], r_send.at[i], r_recv.at[i], nxt)
        for i, (ref, at, n) in enumerate(parts)
    ]
    relay_copies = [
        remote(ref.at[:, own(1)], bounce.at[pl.ds(at, n)], b_send.at[i], b_recv.at[i], flip(0, span))
        for i, (ref, at, n) in enumerate(parts)
    ]
    onward_copies = [
        remote(bounce.at[pl.ds(at, n)], recycled.at[pl.ds(at, n)], o_send.at[i], r_recv.at[i], flip(0, span))
        for i, (ref, at, n) in enumerate(parts)
    ]
    raw_copies = [
        remote(sums, raw_in.at[i], w_send.at[i], w_recv.at[i], device)
        for i, device in enumerate((flip(stream, span), nxt, flip(nxt[0], span)))
    ]
    def each_recycled(act):
        @pl.when(last)
        def _():
            for c in relay_copies:
                act(c)

        @pl.when(jnp.logical_not(last))
        def _():
            for c in r_copies:
                act(c)

    def start(c):
        c.start()

    for c in loads:
        c.wait()

    def sum_rows(o, _):
        for i in range(2):
            for j in range(4):
                cells = x0[2 * o + i, HALF + j, pl.ds(TOP, ROWS), :]
                sums[o, pl.ds(4 * i + j, 1), :] = jnp.sum(cells, axis=0, keepdims=True)
        return 0

    lax.fori_loop(0, 7, sum_rows, 0)
    sums[7] = jnp.zeros((8, NY), jnp.float32)

    for c in raw_copies:
        c.start()
    each_recycled(start)

    @pl.when(jnp.logical_not(first))
    def _():
        for c in z0_copies(0):
            c.start()

    @pl.when(jnp.logical_not(first))
    def _():
        for c in f0_copies() + z0_copies(1):
            c.start()

    @pl.when(gathers)
    def _():
        def tell(i, _):
            device = (stream, ((z + i // 4) % 8) * 8 + ((y + i % 4) % 4) * 2 + xh)
            pl.semaphore_signal(all_here, inc=1, device_id=device, device_id_type=MESH)
            return 0

        lax.fori_loop(1, 32, tell, 0)

    lanes = lax.broadcasted_iota(jnp.int32, (8, NY), 1)
    bottom, top = lanes == 0, lanes == NY - 1

    def chemistry(buf, h):
        def pair(i, _):
            at = h * HALF + 2 * i
            cells = (pl.ds(at, 2), pl.ds(TOP, ROWS), slice(None))
            for s in range(SPECIES):
                picked[s] = buf[(s, *cells)]
            cold = jnp.exp(-buf[(13, *cells)])

            def react(t, acc):
                for u in range(3):
                    r = 3 * t + u
                    rate = jnp.exp(-activation[r] * cold) * picked[table[0, r]] * picked[table[1, r]]
                    acc = tuple(a + weights[r, s] * rate for s, a in enumerate(acc))
                return acc

            zero = jnp.zeros((2, ROWS, NY), jnp.float32)
            acc = lax.fori_loop(0, REACT // 3, react, (zero,) * 10)
            for s in range(SPECIES):
                source[s, pl.ds(at, 2)] = acc[s]
            for s in range(SPECIES, 13):
                source[s, pl.ds(at, 2)] = zero
            source[13, pl.ds(at, 2)] = acc[SPECIES]
            return 0

        lax.fori_loop(0, 2, pair, 0)

    def advance(buf, k, h, store, fields=(0, FIELDS)):
        before, after = BLENDS[k]

        def field(f, _):
            for t in range(2):
                at = TOP + 8 * t
                rows = pl.ds(at, 8)
                mine = [buf[f, p, rows, :] for p in range(PLANES)]
                side = [(ghost if h == 0 else follow.at[k])[f, j, pl.ds(8 * t, 8), :] for j in range(4)]
                line = side + mine if h == 0 else mine + side
                for q in range(HALF):
                    p, c = HALF * h + q, line[4 + q]
                    dx, dz = 0.0, 0.0
                    for o in range(1, 5):
                        dx = dx + STENCIL[o - 1] * (line[4 + q + o] - line[4 + q - o])
                        dz = dz + STENCIL[o - 1] * (buf[f, p, pl.ds(at + o, 8), :] - buf[f, p, pl.ds(at - o, 8), :])
                    down = jnp.where(bottom, 0.0, pltpu.roll(c, 1, 1))
                    up = jnp.where(top, c, pltpu.roll(c, NY - 1, 1))
                    slope = (1.0 + buf[9, p, rows, :]) * dx + buf[11, p, rows, :] * dz
                    change = VISCOSITY * (up - 2.0 * c + down) + source[f, p, pl.ds(8 * t, 8), :] - slope
                    value = after * (c + TIMESTEP * change)
                    if before:
                        value = value + before * x0[f, p, rows, :]
                    store(f, p, t, value)
            return 0

        lax.fori_loop(*fields, field, 0)

    def repeat_last(buf, k):
        @pl.when(last)
        def _():
            def field(f, _):
                for j in range(4):
                    follow[k, f, j] = buf[f, PLANES - 1, pl.ds(TOP, ROWS), :]
                return 0

            lax.fori_loop(0, FIELDS, field, 0)

    for c in small:
        c.wait()

    def weight_row(r, _):
        a, b, p, k = table[0, r], table[1, r], table[2, r], rate_const[r]
        for s in range(SPECIES):
            made = jnp.where(p == s, 2.0 * k, 0.0)
            weights[r, s] = made - jnp.where(a == s, k, 0.0) - jnp.where(b == s, k, 0.0)
        weights[r, SPECIES] = heat[r] * k
        return 0

    lax.fori_loop(0, REACT, weight_row, 0)

    level = lax.broadcasted_iota(jnp.int32, (1, NY), 1).astype(jnp.float32) / (NY - 1.0)
    blend = 0.5 * (1.0 + jnp.tanh(6.0 * (level - 0.5)))
    from_row = lax.broadcasted_iota(jnp.int32, (NY, NY), 0)
    for b, share in enumerate((1.0 - blend, blend)):
        index, frac = index_ref[pl.ds(b, 1), :], frac_ref[pl.ds(b, 1), :]
        lower = jnp.where(from_row == index, (1.0 - frac) * share, 0.0)
        basis[:, pl.ds(b * NY, NY)] = lower + jnp.where(from_row == index + 1, frac * share, 0.0)

    s_copies = [
        remote(both_sums.at[(z + d) % 8], sums_in.at[d - 1], s_send.at[d - 1], s_recv.at[d - 1], along_z(stream, d))
        for d in range(1, 8)
    ]
    p_copies = [remote(part, part_in.at[d - 1], p_send.at[d - 1], p_recv.at[d - 1], along_y(d)) for d in range(1, 4)]
    m_copies = [
        remote(mean_own, mean_in.at[z], m_send.at[d - 1], m_recv.at[d - 1], along_z(stream, d)) for d in range(1, 8)
    ]

    def sums_along_z():
        for c in raw_copies:
            c.wait()
        both_sums[:, 0] = sums[...] + raw_in[0]
        both_sums[:, 1] = raw_in[1] + raw_in[2]

        @pl.when(jnp.logical_not(gathers))
        def _():
            pl.semaphore_wait(all_here, 1)

        for c in s_copies:
            c.start()

    def sums_along_y():
        for c in s_copies:
            c.wait()
        total = both_sums[z]
        for d in range(7):
            total = total + sums_in[d]
        part[...] = total
        for c in p_copies:
            c.start()

    def hand_round():
        for c in p_copies:
            c.wait()
        total = part[...]
        for i in range(3):
            total = total + part_in[i]
        mean_own[...] = total / 1024.0
        mean_in[z] = mean_own[...]
        for c in m_copies:
            c.start()

    chemistry(x0, 0)
    chemistry(x0, 1)
    repeat_last(x0, 0)

    @pl.when(first)
    def _():
        for a, b in zip(relay_copies, onward_copies):
            a.wait_recv()
            b.start()
        for c in z0_copies(0) + z0_copies(1):
            c.start()

    sums_along_z()

    for c in r_copies:
        c.wait_recv()

    for at in range(0, FIELDS, 7):
        cells = recycled[pl.ds(at, 7)].reshape(7 * 4 * ROWS, NY)
        both = jnp.dot(cells, basis[...], precision=lax.Precision.HIGHEST, preferred_element_type=jnp.float32)
        for i in range(7):
            value = both[i * 4 * ROWS:(i + 1) * 4 * ROWS]
            value = fluct_gain[0, at + i] * value[:, :NY] + fluct_gain[1, at + i] * value[:, NY:]
            ghost[at + i] = value.reshape(4, ROWS, NY)

    @pl.when(first)
    def _():
        sums_along_y()

    def rescale_mean(o, _):
        for w in range(2):
            both = jnp.dot(mean_in[o, w], basis[...], precision=lax.Precision.HIGHEST, preferred_element_type=jnp.float32)
            for i in range(2):
                f = 2 * o + i
                gain = [mean_gain[b, f] - fluct_gain[b, f] for b in range(2)]
                rows = both[4 * i:4 * i + 4]
                rows = gain[0] * rows[:, :NY] + gain[1] * rows[:, NY:]
                for q in range(HALF):
                    pull[w, f, pl.ds(q, 1), :] = sum(STENCIL[u - 1] * rows[4 + q - u:5 + q - u] for u in range(q + 1, 5))
                if w == 1:
                    for j in range(4):
                        ghost[f, j] = ghost[f, j] + rows[j:j + 1]
        return 0

    def correct_early(blocks):
        factor = [[TIMESTEP * (1.0 + x0[9, q, rows, :]) for rows in blocks] for q in range(HALF)]

        def field(f, _):
            for q in range(HALF):
                for t, rows in enumerate(blocks):
                    x1[f, q, rows, :] = early[f, q, rows, :] + factor[q][t] * pull[1, f, pl.ds(q, 1), :]
            return 0

        lax.fori_loop(0, FIELDS, field, 0)

    def correct_follow():
        @pl.when(jnp.logical_not(last))
        def _():
            factor = [TIMESTEP * (1.0 + follow[0, 9, q]) for q in range(HALF)]

            def field(f, _):
                for q in range(HALF):
                    follow[1, f, q] = follow[1, f, q] + factor[q] * pull[0, f, pl.ds(q, 1), :]
                return 0

            lax.fori_loop(0, FIELDS, field, 0)

    def receive(copies):
        for c in copies:
            c.wait_recv()

    buffers = (x0, x1, x2)
    for k in range(3):
        buf = buffers[k]
        target = buffers[k + 1] if k < 2 else None
        for h in range(2):
            if (k, h) == (1, 0):
                for c in m_copies:
                    c.wait()
                lax.fori_loop(0, 7, rescale_mean, 0)
                correct_early([pl.ds(TOP, 8), pl.ds(TOP + 8, 8)])
                chemistry(x1, 0)
            receive(z0_copies(h) if k == 0 else z_copies(buf, k - 1, h))
            if (k, h) == (1, 0):
                correct_early([pl.ds(TOP - 4, 4), pl.ds(TOP + ROWS, 4)])
            if h == 1:

                @pl.when(jnp.logical_not(last))
                def _():
                    receive(f0_copies() if k == 0 else [f_copy(buf, k - 1)])

                if k == 1:
                    correct_follow()

            if k < 2:
                into = early if (k, h) == (0, 0) else target

                def store(f, p, t, value):
                    into[f, p, pl.ds(TOP + 8 * t, 8), :] = value

                advance(buf, k, h, store)
                for c in z_copies(target, k, h):
                    c.start()
                if h == 0:

                    @pl.when(jnp.logical_not(first))
                    def _():
                        f_copy(target, k).start()

                if (k, h) == (0, 0):

                    @pl.when(jnp.logical_not(first))
                    def _():
                        sums_along_y()

                    @pl.when(first | (z >= 1))
                    def _():
                        hand_round()

                if (k, h) == (0, 1):

                    @pl.when(jnp.logical_not(first | (z >= 1)))
                    def _():
                        hand_round()

                if (k, h) != (0, 0):
                    chemistry(target, h)
                if h == 1:
                    repeat_last(target, k + 1)
            else:

                def store_species(f, p, t, value):
                    species_out[f, p, pl.ds(8 * t, 8), :] = value

                def store_flow(f, p, t, value):
                    flow_out[f - SPECIES, p, pl.ds(8 * t, 8), :] = value

                advance(buf, k, h, store_species, (0, SPECIES))
                advance(buf, k, h, store_flow, (SPECIES, FIELDS))

    for h in range(2):
        for c in z0_copies(h) + z_copies(x1, 0, h) + z_copies(x2, 1, h):
            c.wait_send()
    each_recycled(lambda c: c.wait_send())

    @pl.when(first)
    def _():
        for c in onward_copies:
            c.wait_send()

    @pl.when(jnp.logical_not(first))
    def _():
        for c in f0_copies() + [f_copy(x1, 0), f_copy(x2, 1)]:
            c.wait_send()


def hand_out(species, flow, species_out, flow_out, sem):
    copies = [
        pltpu.make_async_copy(a.at[:, own(h)], b.at[:, own(h)], sem.at[i, h])
        for i, (a, b) in enumerate(((species, species_out), (flow, flow_out)))
        for h in range(2)
    ]
    for c in copies:
        c.start()
    for c in copies:
        c.wait()


def on_device(species, flow, index, frac, mean_gain, fluct_gain, table, rate_const, activation, heat):
    vmem, hbm = (pl.BlockSpec(memory_space=m) for m in (pltpu.VMEM, pltpu.HBM))
    f32, dma = jnp.float32, pltpu.SemaphoreType.DMA
    extended = pltpu.VMEM((FIELDS, PLANES, 2 * TOP + ROWS, NY), f32)
    small = (index, frac, mean_gain, fluct_gain, table.T, rate_const, activation, heat)
    scratch = [(pltpu.VMEM if i < 2 else pltpu.SMEM)(a.shape, a.dtype) for i, a in enumerate(small)]
    scratch += [
        extended, extended, extended,
        pltpu.VMEM((FIELDS, HALF, 2 * TOP + ROWS, NY), f32),
        pltpu.VMEM((3, FIELDS, HALF, ROWS, NY), f32),
        pltpu.VMEM((FIELDS, HALF, ROWS, NY), f32),
        pltpu.VMEM((FIELDS, HALF, ROWS, NY), f32),
        pltpu.VMEM((FIELDS, PLANES, ROWS, NY), f32),
        pltpu.VMEM((SPECIES, 2, ROWS, NY), f32),
        pltpu.SMEM((REACT, SPECIES + 1), f32),
        pltpu.VMEM((NY, 2 * NY), f32),
        pltpu.VMEM((2, FIELDS, HALF, NY), f32),
        pltpu.VMEM((8, 8, NY), f32),
        pltpu.VMEM((3, 8, 8, NY), f32),
        pltpu.VMEM((8, 2, 8, NY), f32),
        pltpu.VMEM((7, 2, 8, NY), f32),
        pltpu.VMEM((2, 8, NY), f32),
        pltpu.VMEM((3, 2, 8, NY), f32),
        pltpu.VMEM((2, 8, NY), f32),
        pltpu.VMEM((8, 2, 8, NY), f32),
        pltpu.VMEM((FIELDS, HALF, ROWS, NY), f32),
        dma((2,)), dma((8,)),
        dma((2, 2, 2)), dma((2, 2, 2)), dma((2, 2, 2)), dma((2, 2, 2)),
        dma((2,)), dma((2,)), dma((2,)), dma((2,)), dma((2,)), dma((2,)),
        dma((3,)), dma((3,)), dma((7,)), dma((7,)), dma((3,)), dma((3,)), dma((7,)), dma((7,)),
        dma((2,)), dma((2,)), dma((2,)), pltpu.SemaphoreType.REGULAR,
    ]
    results = pl.pallas_call(
        kernel,
        out_shape=(pltpu.VMEM(species.shape, f32), pltpu.VMEM(flow.shape, f32)),
        in_specs=[hbm] * 10,
        out_specs=(vmem, vmem),
        scratch_shapes=scratch,
        compiler_params=pltpu.CompilerParams(
            collective_id=0, has_side_effects=True, vmem_limit_bytes=60 * 1024 * 1024
        ),
    )(species, flow, *small)
    return pl.pallas_call(
        hand_out,
        out_shape=tuple(jax.ShapeDtypeStruct(a.shape, f32) for a in results),
        in_specs=[vmem] * 2,
        out_specs=(hbm, hbm),
        scratch_shapes=[dma((2, 2))],
    )(*(pltpu.with_memory_space_constraint(a, pltpu.VMEM) for a in results))


def solution(mesh):
    split = P(None, "stream", "span", None)
    return jax.shard_map(
        on_device, mesh=mesh, in_specs=(split, split) + (P(),) * 8, out_specs=(split, split), check_vma=False
    )
```

```python
import functools

import jax
import jax.numpy as jnp
from jax import lax
from jax.experimental import pallas as pl
from jax.experimental.pallas import tpu as pltpu
from jax.sharding import PartitionSpec as P

MESH = pl.DeviceIdType.MESH
STENCIL = (0.8, -0.2, 4.0 / 105.0, -1.0 / 280.0)
TIMESTEP = 0.2
VISCOSITY = 0.1
SPECIES, FIELDS, REACT = 9, 14, 21
NY, ROWS, PLANES, HALF = 128, 16, 8, 4
GATHER_Z, GATHER_Y = 7, 2
TOP = 8
BLENDS = ((0.0, 1.0), (0.75, 0.25), (1.0 / 3.0, 2.0 / 3.0))


def own(h):
    return pl.ds(h * HALF, HALF)


def kernel(
    species_ref, flow_ref, index_hbm, frac_hbm, mean_gain_hbm, fluct_gain_hbm, table_hbm, rate_const_hbm, activation_hbm, heat_hbm,
    species_out, flow_out, index_ref, frac_ref, mean_gain, fluct_gain, table, rate_const, activation, heat,
    x0, x1, x2, early, follow, recycled, ghost, source, picked, weights, basis, pull,
    sums, raw_in, both_sums, sums_in, part, part_in, mean_own, mean_in, bounce,
    load_sem, small_sem, z_send, z_recv, z0_send, z0_recv, f_send, f_recv, f0_send, f0_recv, r_send, r_recv,
    w_send, w_recv, s_send, s_recv, p_send, p_recv, m_send, m_recv, b_send, b_recv, o_send, all_here,
):
    stream, span = lax.axis_index("stream"), lax.axis_index("span")
    z, y, xh = span // 8, (span // 2) % 4, span % 2
    right, left = (stream, (span + 1) % 64), (stream, (span + 63) % 64)
    nxt, prev = ((stream + 1) % 4, span), ((stream + 3) % 4, span)
    first, last = stream == 0, stream == 3

    def along_z(group, d):
        return (group, ((z + d) % 8) * 8 + y * 2 + xh)

    def along_y(d):
        return (stream, z * 8 + ((y + d) % 4) * 2 + xh)

    def flip(group, at):
        return (group, at + 1 - 2 * (at % 2))

    gatherer = (stream, GATHER_Z * 8 + GATHER_Y * 2 + xh)
    gathers = span == gatherer[1]

    barrier = pltpu.get_barrier_semaphore()

    def hello(device):
        pl.semaphore_signal(barrier, inc=1, device_id=device, device_id_type=MESH)

    hello(left)
    hello(right)
    hello(prev)
    hello(flip(prev[0], span))
    hello(flip(stream, span))

    @pl.when(jnp.logical_not(gathers))
    def _():
        hello(gatherer)

    @pl.when(jnp.logical_not(last))
    def _():
        hello(nxt)

    loads = [
        pltpu.make_async_copy(species_ref, x0.at[pl.ds(0, SPECIES), :, pl.ds(TOP, ROWS)], load_sem.at[0]),
        pltpu.make_async_copy(flow_ref, x0.at[pl.ds(SPECIES, 5), :, pl.ds(TOP, ROWS)], load_sem.at[1]),
    ]
    for c in loads:
        c.start()

    small_from = (index_hbm, frac_hbm, mean_gain_hbm, fluct_gain_hbm, table_hbm, rate_const_hbm, activation_hbm, heat_hbm)
    small_to = (index_ref, frac_ref, mean_gain, fluct_gain, table, rate_const, activation, heat)
    small = [pltpu.make_async_copy(a, b, small_sem.at[i]) for i, (a, b) in enumerate(zip(small_from, small_to))]
    for c in small:
        c.start()

    pl.semaphore_wait(barrier, 2 + 3 + jnp.where(first, 0, 1) + jnp.where(gathers, 31, 0))

    def remote(src, dst, send, recv, device):
        return pltpu.make_async_remote_copy(
            src_ref=src, dst_ref=dst, send_sem=send, recv_sem=recv, device_id=device, device_id_type=MESH
        )

    parts = ((species_ref, 0, SPECIES), (flow_ref, SPECIES, 5))

    def z0_copies(h):
        return [
            remote(ref.at[:, own(h), pl.ds(0, 4)], x0.at[pl.ds(at, n), own(h), pl.ds(TOP + ROWS, 4)],
                   z0_send.at[h, i, 0], z0_recv.at[h, i, 0], left)
            for i, (ref, at, n) in enumerate(parts)
        ] + [
            remote(ref.at[:, own(h), pl.ds(ROWS - 4, 4)], x0.at[pl.ds(at, n), own(h), pl.ds(TOP - 4, 4)],
                   z0_send.at[h, i, 1], z0_recv.at[h, i, 1], right)
            for i, (ref, at, n) in enumerate(parts)
        ]

    def z_copies(buf, k, h):
        if (k, h) == (0, 0):
            buf = early
        return [
            remote(buf.at[:, own(h), pl.ds(TOP + ROWS - 4, 4)], buf.at[:, own(h), pl.ds(TOP - 4, 4)],
                   z_send.at[k, h, 1], z_recv.at[k, h, 1], right),
            remote(buf.at[:, own(h), pl.ds(TOP, 4)], buf.at[:, own(h), pl.ds(TOP + ROWS, 4)],
                   z_send.at[k, h, 0], z_recv.at[k, h, 0], left),
        ]

    def f0_copies():
        return [
            remote(ref.at[:, own(0)], follow.at[0, pl.ds(at, n)], f0_send.at[i], f0_recv.at[i], prev)
            for i, (ref, at, n) in enumerate(parts)
        ]

    def f_copy(buf, k):
        if k == 0:
            buf = early
        return remote(buf.at[:, own(0), pl.ds(TOP, ROWS)], follow.at[k + 1], f_send.at[k], f_recv.at[k], prev)

    r_copies = [
        remote(ref.at[:, own(1)], recycled.at[pl.ds(at, n)], r_send.at[i], r_recv.at[i], nxt)
        for i, (ref, at, n) in enumerate(parts)
    ]
    relay_copies = [
        remote(ref.at[:, own(1)], bounce.at[pl.ds(at, n)], b_send.at[i], b_recv.at[i], flip(0, span))
        for i, (ref, at, n) in enumerate(parts)
    ]
    onward_copies = [
        remote(bounce.at[pl.ds(at, n)], recycled.at[pl.ds(at, n)], o_send.at[i], r_recv.at[i], flip(0, span))
        for i, (ref, at, n) in enumerate(parts)
    ]
    raw_copies = [
        remote(sums, raw_in.at[i], w_send.at[i], w_recv.at[i], device)
        for i, device in enumerate((flip(stream, span), nxt, flip(nxt[0], span)))
    ]
    def each_recycled(act):
        @pl.when(last)
        def _():
            for c in relay_copies:
                act(c)

        @pl.when(jnp.logical_not(last))
        def _():
            for c in r_copies:
                act(c)

    def start(c):
        c.start()

    for c in loads:
        c.wait()

    def sum_rows(o, _):
        for i in range(2):
            for j in range(4):
                cells = x0[2 * o + i, HALF + j, pl.ds(TOP, ROWS), :]
                sums[o, pl.ds(4 * i + j, 1), :] = jnp.sum(cells, axis=0, keepdims=True)
        return 0

    lax.fori_loop(0, 7, sum_rows, 0)
    sums[7] = jnp.zeros((8, NY), jnp.float32)

    for c in raw_copies:
        c.start()
    each_recycled(start)

    @pl.when(jnp.logical_not(first))
    def _():
        for c in z0_copies(0):
            c.start()

    @pl.when(jnp.logical_not(first))
    def _():
        for c in f0_copies() + z0_copies(1):
            c.start()

    @pl.when(gathers)
    def _():
        def tell(i, _):
            device = (stream, ((z + i // 4) % 8) * 8 + ((y + i % 4) % 4) * 2 + xh)
            pl.semaphore_signal(all_here, inc=1, device_id=device, device_id_type=MESH)
            return 0

        lax.fori_loop(1, 32, tell, 0)

    lanes = lax.broadcasted_iota(jnp.int32, (8, NY), 1)
    bottom, top = lanes == 0, lanes == NY - 1

    def chemistry(buf, h):
        def pair(i, _):
            at = h * HALF + 2 * i
            cells = (pl.ds(at, 2), pl.ds(TOP, ROWS), slice(None))
            for s in range(SPECIES):
                picked[s] = buf[(s, *cells)]
            cold = jnp.exp(-buf[(13, *cells)])

            def react(t, acc):
                for u in range(3):
                    r = 3 * t + u
                    rate = jnp.exp(-activation[r] * cold) * picked[table[0, r]] * picked[table[1, r]]
                    acc = tuple(a + weights[r, s] * rate for s, a in enumerate(acc))
                return acc

            zero = jnp.zeros((2, ROWS, NY), jnp.float32)
            acc = lax.fori_loop(0, REACT // 3, react, (zero,) * 10)
            for s in range(SPECIES):
                source[s, pl.ds(at, 2)] = acc[s]
            for s in range(SPECIES, 13):
                source[s, pl.ds(at, 2)] = zero
            source[13, pl.ds(at, 2)] = acc[SPECIES]
            return 0

        lax.fori_loop(0, 2, pair, 0)

    def advance(buf, k, h, store, fields=(0, FIELDS)):
        before, after = BLENDS[k]

        def field(f, _):
            for t in range(2):
                at = TOP + 8 * t
                rows = pl.ds(at, 8)
                mine = [buf[f, p, rows, :] for p in range(PLANES)]
                side = [(ghost if h == 0 else follow.at[k])[f, j, pl.ds(8 * t, 8), :] for j in range(4)]
                line = side + mine if h == 0 else mine + side
                for q in range(HALF):
                    p, c = HALF * h + q, line[4 + q]
                    dx, dz = 0.0, 0.0
                    for o in range(1, 5):
                        dx = dx + STENCIL[o - 1] * (line[4 + q + o] - line[4 + q - o])
                        dz = dz + STENCIL[o - 1] * (buf[f, p, pl.ds(at + o, 8), :] - buf[f, p, pl.ds(at - o, 8), :])
                    down = jnp.where(bottom, 0.0, pltpu.roll(c, 1, 1))
                    up = jnp.where(top, c, pltpu.roll(c, NY - 1, 1))
                    slope = (1.0 + buf[9, p, rows, :]) * dx + buf[11, p, rows, :] * dz
                    change = VISCOSITY * (up - 2.0 * c + down) + source[f, p, pl.ds(8 * t, 8), :] - slope
                    value = after * (c + TIMESTEP * change)
                    if before:
                        value = value + before * x0[f, p, rows, :]
                    store(f, p, t, value)
            return 0

        lax.fori_loop(*fields, field, 0)

    def repeat_last(buf, k):
        @pl.when(last)
        def _():
            def field(f, _):
                for j in range(4):
                    follow[k, f, j] = buf[f, PLANES - 1, pl.ds(TOP, ROWS), :]
                return 0

            lax.fori_loop(0, FIELDS, field, 0)

    for c in small:
        c.wait()

    def weight_row(r, _):
        a, b, p, k = table[0, r], table[1, r], table[2, r], rate_const[r]
        for s in range(SPECIES):
            made = jnp.where(p == s, 2.0 * k, 0.0)
            weights[r, s] = made - jnp.where(a == s, k, 0.0) - jnp.where(b == s, k, 0.0)
        weights[r, SPECIES] = heat[r] * k
        return 0

    lax.fori_loop(0, REACT, weight_row, 0)

    level = lax.broadcasted_iota(jnp.int32, (1, NY), 1).astype(jnp.float32) / (NY - 1.0)
    blend = 0.5 * (1.0 + jnp.tanh(6.0 * (level - 0.5)))
    from_row = lax.broadcasted_iota(jnp.int32, (NY, NY), 0)
    for b, share in enumerate((1.0 - blend, blend)):
        index, frac = index_ref[pl.ds(b, 1), :], frac_ref[pl.ds(b, 1), :]
        lower = jnp.where(from_row == index, (1.0 - frac) * share, 0.0)
        basis[:, pl.ds(b * NY, NY)] = lower + jnp.where(from_row == index + 1, frac * share, 0.0)

    s_copies = [
        remote(both_sums.at[(z + d) % 8], sums_in.at[d - 1], s_send.at[d - 1], s_recv.at[d - 1], along_z(stream, d))
        for d in range(1, 8)
    ]
    p_copies = [remote(part, part_in.at[d - 1], p_send.at[d - 1], p_recv.at[d - 1], along_y(d)) for d in range(1, 4)]
    m_copies = [
        remote(mean_own, mean_in.at[z], m_send.at[d - 1], m_recv.at[d - 1], along_z(stream, d)) for d in range(1, 8)
    ]

    def sums_along_z():
        for c in raw_copies:
            c.wait()
        both_sums[:, 0] = sums[...] + raw_in[0]
        both_sums[:, 1] = raw_in[1] + raw_in[2]

        @pl.when(jnp.logical_not(gathers))
        def _():
            pl.semaphore_wait(all_here, 1)

        for c in s_copies:
            c.start()

    def sums_along_y():
        for c in s_copies:
            c.wait()
        total = both_sums[z]
        for d in range(7):
            total = total + sums_in[d]
        part[...] = total
        for c in p_copies:
            c.start()

    def hand_round():
        for c in p_copies:
            c.wait()
        total = part[...]
        for i in range(3):
            total = total + part_in[i]
        mean_own[...] = total / 1024.0
        mean_in[z] = mean_own[...]
        for c in m_copies:
            c.start()

    chemistry(x0, 0)

    @pl.when(first)
    def _():
        for a, b in zip(relay_copies, onward_copies):
            a.wait_recv()
            b.start()
        for c in z0_copies(0) + z0_copies(1):
            c.start()

    chemistry(x0, 1)
    repeat_last(x0, 0)
    sums_along_z()

    for c in r_copies:
        c.wait_recv()

    for at in range(0, FIELDS, 7):
        cells = recycled[pl.ds(at, 7)].reshape(7 * 4 * ROWS, NY)
        both = jnp.dot(cells, basis[...], precision=lax.Precision.HIGHEST, preferred_element_type=jnp.float32)
        for i in range(7):
            value = both[i * 4 * ROWS:(i + 1) * 4 * ROWS]
            value = fluct_gain[0, at + i] * value[:, :NY] + fluct_gain[1, at + i] * value[:, NY:]
            ghost[at + i] = value.reshape(4, ROWS, NY)

    @pl.when(first)
    def _():
        sums_along_y()

    def rescale_mean(o, _):
        for w in range(2):
            both = jnp.dot(mean_in[o, w], basis[...], precision=lax.Precision.HIGHEST, preferred_element_type=jnp.float32)
            for i in range(2):
                f = 2 * o + i
                gain = [mean_gain[b, f] - fluct_gain[b, f] for b in range(2)]
                rows = both[4 * i:4 * i + 4]
                rows = gain[0] * rows[:, :NY] + gain[1] * rows[:, NY:]
                for q in range(HALF):
                    pull[w, f, pl.ds(q, 1), :] = sum(STENCIL[u - 1] * rows[4 + q - u:5 + q - u] for u in range(q + 1, 5))
                if w == 1:
                    for j in range(4):
                        ghost[f, j] = ghost[f, j] + rows[j:j + 1]
        return 0

    def correct_early(blocks):
        factor = [[TIMESTEP * (1.0 + x0[9, q, rows, :]) for rows in blocks] for q in range(HALF)]

        def field(f, _):
            for q in range(HALF):
                for t, rows in enumerate(blocks):
                    x1[f, q, rows, :] = early[f, q, rows, :] + factor[q][t] * pull[1, f, pl.ds(q, 1), :]
            return 0

        lax.fori_loop(0, FIELDS, field, 0)

    def correct_follow():
        @pl.when(jnp.logical_not(last))
        def _():
            factor = [TIMESTEP * (1.0 + follow[0, 9, q]) for q in range(HALF)]

            def field(f, _):
                for q in range(HALF):
                    follow[1, f, q] = follow[1, f, q] + factor[q] * pull[0, f, pl.ds(q, 1), :]
                return 0

            lax.fori_loop(0, FIELDS, field, 0)

    def receive(copies):
        for c in copies:
            c.wait_recv()

    buffers = (x0, x1, x2)
    for k in range(3):
        buf = buffers[k]
        target = buffers[k + 1] if k < 2 else None
        for h in range(2):
            if (k, h) == (1, 0):
                for c in m_copies:
                    c.wait()
                lax.fori_loop(0, 7, rescale_mean, 0)
                correct_early([pl.ds(TOP, 8), pl.ds(TOP + 8, 8)])
                chemistry(x1, 0)
            receive(z0_copies(h) if k == 0 else z_copies(buf, k - 1, h))
            if (k, h) == (1, 0):
                correct_early([pl.ds(TOP - 4, 4), pl.ds(TOP + ROWS, 4)])
            if h == 1:

                @pl.when(jnp.logical_not(last))
                def _():
                    receive(f0_copies() if k == 0 else [f_copy(buf, k - 1)])

                if k == 1:
                    correct_follow()

            if k < 2:
                into = early if (k, h) == (0, 0) else target

                def store(f, p, t, value):
                    into[f, p, pl.ds(TOP + 8 * t, 8), :] = value

                advance(buf, k, h, store)
                for c in z_copies(target, k, h):
                    c.start()
                if h == 0:

                    @pl.when(jnp.logical_not(first))
                    def _():
                        f_copy(target, k).start()

                if (k, h) == (0, 0):

                    @pl.when(jnp.logical_not(first))
                    def _():
                        sums_along_y()

                    @pl.when(first | (z >= 1))
                    def _():
                        hand_round()

                if (k, h) == (0, 1):

                    @pl.when(jnp.logical_not(first | (z >= 1)))
                    def _():
                        hand_round()

                if (k, h) != (0, 0):
                    chemistry(target, h)
                if h == 1:
                    repeat_last(target, k + 1)
            else:

                def store_species(f, p, t, value):
                    species_out[f, p, pl.ds(8 * t, 8), :] = value

                def store_flow(f, p, t, value):
                    flow_out[f - SPECIES, p, pl.ds(8 * t, 8), :] = value

                advance(buf, k, h, store_species, (0, SPECIES))
                advance(buf, k, h, store_flow, (SPECIES, FIELDS))

    for h in range(2):
        for c in z0_copies(h) + z_copies(x1, 0, h) + z_copies(x2, 1, h):
            c.wait_send()
    each_recycled(lambda c: c.wait_send())

    @pl.when(first)
    def _():
        for c in onward_copies:
            c.wait_send()

    @pl.when(jnp.logical_not(first))
    def _():
        for c in f0_copies() + [f_copy(x1, 0), f_copy(x2, 1)]:
            c.wait_send()


def hand_out(species, flow, species_out, flow_out, sem):
    copies = [
        pltpu.make_async_copy(a.at[:, own(h)], b.at[:, own(h)], sem.at[i, h])
        for i, (a, b) in enumerate(((species, species_out), (flow, flow_out)))
        for h in range(2)
    ]
    for c in copies:
        c.start()
    for c in copies:
        c.wait()


def on_device(species, flow, index, frac, mean_gain, fluct_gain, table, rate_const, activation, heat):
    vmem, hbm = (pl.BlockSpec(memory_space=m) for m in (pltpu.VMEM, pltpu.HBM))
    f32, dma = jnp.float32, pltpu.SemaphoreType.DMA
    extended = pltpu.VMEM((FIELDS, PLANES, 2 * TOP + ROWS, NY), f32)
    small = (index, frac, mean_gain, fluct_gain, table.T, rate_const, activation, heat)
    scratch = [(pltpu.VMEM if i < 2 else pltpu.SMEM)(a.shape, a.dtype) for i, a in enumerate(small)]
    scratch += [
        extended, extended, extended,
        pltpu.VMEM((FIELDS, HALF, 2 * TOP + ROWS, NY), f32),
        pltpu.VMEM((3, FIELDS, HALF, ROWS, NY), f32),
        pltpu.VMEM((FIELDS, HALF, ROWS, NY), f32),
        pltpu.VMEM((FIELDS, HALF, ROWS, NY), f32),
        pltpu.VMEM((FIELDS, PLANES, ROWS, NY), f32),
        pltpu.VMEM((SPECIES, 2, ROWS, NY), f32),
        pltpu.SMEM((REACT, SPECIES + 1), f32),
        pltpu.VMEM((NY, 2 * NY), f32),
        pltpu.VMEM((2, FIELDS, HALF, NY), f32),
        pltpu.VMEM((8, 8, NY), f32),
        pltpu.VMEM((3, 8, 8, NY), f32),
        pltpu.VMEM((8, 2, 8, NY), f32),
        pltpu.VMEM((7, 2, 8, NY), f32),
        pltpu.VMEM((2, 8, NY), f32),
        pltpu.VMEM((3, 2, 8, NY), f32),
        pltpu.VMEM((2, 8, NY), f32),
        pltpu.VMEM((8, 2, 8, NY), f32),
        pltpu.VMEM((FIELDS, HALF, ROWS, NY), f32),
        dma((2,)), dma((8,)),
        dma((2, 2, 2)), dma((2, 2, 2)), dma((2, 2, 2)), dma((2, 2, 2)),
        dma((2,)), dma((2,)), dma((2,)), dma((2,)), dma((2,)), dma((2,)),
        dma((3,)), dma((3,)), dma((7,)), dma((7,)), dma((3,)), dma((3,)), dma((7,)), dma((7,)),
        dma((2,)), dma((2,)), dma((2,)), pltpu.SemaphoreType.REGULAR,
    ]
    results = pl.pallas_call(
        kernel,
        out_shape=(pltpu.VMEM(species.shape, f32), pltpu.VMEM(flow.shape, f32)),
        in_specs=[hbm] * 10,
        out_specs=(vmem, vmem),
        scratch_shapes=scratch,
        compiler_params=pltpu.CompilerParams(
            collective_id=0, has_side_effects=True, vmem_limit_bytes=60 * 1024 * 1024
        ),
    )(species, flow, *small)
    return pl.pallas_call(
        hand_out,
        out_shape=tuple(jax.ShapeDtypeStruct(a.shape, f32) for a in results),
        in_specs=[vmem] * 2,
        out_specs=(hbm, hbm),
        scratch_shapes=[dma((2, 2))],
    )(*(pltpu.with_memory_space_constraint(a, pltpu.VMEM) for a in results))


def solution(mesh):
    split = P(None, "stream", "span", None)
    return jax.shard_map(
        on_device, mesh=mesh, in_specs=(split, split) + (P(),) * 8, out_specs=(split, split), check_vma=False
    )
```
